32 devices in a mesh: section: 2 (over core), expert: 8 (over z, x), dp: 2 (over y).
Axes of the slice: x: 2, y: 2, z: 4, core: 2. Of those that a mesh axis runs over, the one named last changes fastest.
Arguments:
- boundary: bfloat16 [2, 2, 2048, 1536], P('section', None, ('expert', 'dp')), may hold values from -6 to 6
- w_query: bfloat16 [2, 1536, 1536], P('section'), may hold values from -0.15625 to 0.15625
- w_key: bfloat16 [2, 1536, 256], P('section'), may hold values from -0.15625 to 0.15625
- w_value: bfloat16 [2, 1536, 256], P('section'), may hold values from -0.15625 to 0.15625
- w_out: bfloat16 [2, 1536, 1536], P('section'), may hold values from -0.625 to 0.625
- norm_attn: float32 [2, 1536], P('section'), may hold values from 0.5 to 1.5
- norm_ffn: float32 [2, 1536], P('section'), may hold values from 0.5 to 1.5
- w_gate: bfloat16 [2, 8, 1536, 768], P('section', 'expert'), may hold values from -0.15625 to 0.15625
- w_up: bfloat16 [2, 8, 1536, 768], P('section', 'expert'), may hold values from -0.15625 to 0.15625
- w_down: bfloat16 [2, 8, 768, 1536], P('section', 'expert'), may hold values from -0.4375 to 0.4375
- expert_ids: int32 [2, 2, 2048, 4], P('section', None, ('expert', 'dp')), may hold values from 0 to 7, all different within a row; in each aligned block of 128 rows (0 to 127, 128 to 255, ..., all dimensions but the last counted through in order) at most 96 rows name the same one
- route_weights: float32 [2, 2, 2048, 4], P('section', None, ('expert', 'dp')), may hold values from 0.15 to 0.35
- segments: int32 [2, 2048], P(None, 'expert'), may hold values from 0 to 15, as said below
Outputs:
- activations: bfloat16 [2, 2, 2048, 1536], P('section', None, ('expert', 'dp'))
- input_grads: bfloat16 [2, 2, 2048, 1536], P('section', None, ('expert', 'dp'))
- grad_query: float32 [2, 1536, 1536], P('section')
- grad_key: float32 [2, 1536, 256], P('section')
- grad_value: float32 [2, 1536, 256], P('section')
- grad_out: float32 [2, 1536, 1536], P('section')
- grad_norm_attn: float32 [2, 1536], P('section')
- grad_norm_ffn: float32 [2, 1536], P('section')
- grad_gate: float32 [2, 8, 1536, 768], P('section', 'expert', 'dp')
- grad_up: float32 [2, 8, 1536, 768], P('section', 'expert', 'dp')
- grad_down: float32 [2, 8, 768, 1536], P('section', 'expert', None, 'dp')
The draws below stay inside these ranges and needn't reach their ends.
Inputs may be any that keep to these rules, and one draw needn't show every extreme that they name: `expert_ids`: each token names 4 different experts. Among the 128 tokens of one device block (aligned blocks of tokens of one layer and micro-batch) no expert is named by more than 96 tokens, a bound that some block reaches. `segments`: ids never fall along the tokens of a micro-batch. Sequence s of 256 tokens holds either document 2 s alone or documents 2 s and 2 s + 1, each of 100 tokens or more; for each sequence, one micro-batch drawn from the seed holds document 2 s alone.
All inputs are finite; a program needn't handle non-finite values.
Results may differ from the reference program's by a relative error of at most 0.03.
Values may be sent and summed in bfloat16 or wider, within the bound.
A program may use at most 192 MiB of HBM per device.

```python
import math
import jax
import jax.numpy as jnp
import numpy as np
from jax import lax

D = 1536
HEADS = 12
KV_HEADS = 2
HEAD_DIM = 128
FF = 768
TOP = 4
TOK_MB = 128
MICRO = 2
LAYERS = 2
EXPERTS = 8
SEQ = 256
TOKENS = 2048
CAP = 96


def draw_segments(key, part):
    key = jax.random.fold_in(key, 11)
    cut_key, pick_key = jax.random.split(key)
    seq_count = TOKENS // SEQ
    cuts = jax.random.randint(cut_key, (MICRO, seq_count, 1), 25 * SEQ // 64, 39 * SEQ // 64 + 1)
    whole_micro = jax.random.randint(pick_key, (1, seq_count, 1), 0, MICRO)
    split_flag = (jnp.arange(MICRO, dtype=jnp.int32)[:, None, None] != whole_micro).astype(jnp.int32)
    places = jnp.arange(SEQ, dtype=jnp.int32)[None, None, :]
    within = (places >= cuts).astype(jnp.int32) * split_flag
    offsets = 2 * jnp.arange(seq_count, dtype=jnp.int32)[None, :, None]
    return (within + offsets).reshape(MICRO, TOKENS).astype(jnp.int32)


def levels(own_key, dims, cuts, smallest, largest):
    gain, own = 1.0, jax.random.fold_in(own_key, 6)
    for dim, blocks in cuts:
        draws = jnp.exp(jax.random.uniform(jax.random.fold_in(own, dim), (blocks,), jnp.float32, smallest / len(cuts), largest / len(cuts)))
        gain = gain * jnp.repeat(draws, dims[dim] // blocks).reshape([-1 if axis == dim else 1 for axis in range(len(dims))])
    return gain


def routed_block(rng, own, number, rows, amount, top, bound, lean):
    sequence = jax.random.permutation(rng, amount)
    packed, ordinary = shares(amount, rows * top, bound, lean, True), shares(amount, rows * top, bound, lean, False)
    places = jnp.arange(amount)

    def named(sizes, offset_by):
        used = int((sizes > 0).sum())
        fixed = max(1, used // 4)
        moved = fixed + (places - fixed + offset_by * (used - fixed)) % max(1, amount - fixed)
        return jnp.zeros((amount,), jnp.int32).at[sequence[jnp.where(places < fixed, places, moved)]].set(jnp.asarray(sizes, jnp.int32))

    sizes = jnp.where(number % 4 == 0, named(packed, number // 4), named(ordinary, number - number // 4 - 1))
    mixed = jax.random.permutation(jax.random.fold_in(own, 3), amount)
    donor, taker = mixed[0:amount // 2 * 2:2], mixed[1:amount // 2 * 2:2]
    margin = jnp.minimum(sizes[donor] - 1, bound - sizes[taker]) // 2
    margin = jnp.where((donor == sequence[0]) | (taker == sequence[0]) | (sizes[taker] == 0), 0, jnp.maximum(margin, 0))
    moved = jax.random.randint(jax.random.fold_in(own, 4), (amount // 2,), 0, 1 << 20) % (margin + 1)
    sizes = sizes.at[donor].add(-moved).at[taker].add(moved)
    members = jnp.searchsorted(jnp.cumsum(sizes), jnp.arange(rows * top), side="right").astype(jnp.int32)
    grid = members.reshape(top, rows).T
    grid = grid[jax.random.permutation(jax.random.fold_in(own, 1), rows)]
    offset_by = jax.random.randint(jax.random.fold_in(own, 2), (rows, 1), 0, top)
    return jnp.take_along_axis(grid, (jnp.arange(top)[None, :] + offset_by) % top, axis=1)


def shares(number_of, total, limit, slope, full):
    loads = [(1 << 20) // math.isqrt(rank ** slope) + 1 for rank in range(1, number_of + 1)]
    largest = limit if full else min(limit, max(-(-total // number_of), total * loads[0] // sum(loads)))
    least = 1 if total - largest >= number_of - 1 else 0
    counts, surplus = [largest] + [least] * (number_of - 1), total - largest - least * (number_of - 1)
    while surplus > 0:
        candidates = [i for i in range(1, number_of) if counts[i] < largest] or [i for i in range(1, number_of) if counts[i] < limit]
        mass, left = sum([loads[i] for i in candidates]), surplus
        for i in candidates:
            addition = min(limit - counts[i], max(1, left * loads[i] // mass), surplus)
            counts[i] = counts[i] + addition
            surplus = surplus - addition
    return np.array(counts)


def centred(stream_key, extent, width, reach, cuts=(), held_as=jnp.bfloat16):
    drawn = jax.random.normal(stream_key, extent, jnp.float32) * width
    if len(cuts) > 0:
        drawn = levels(stream_key, extent, cuts, -0.22, 0.18) * drawn
    return jnp.clip(drawn, min=-reach, max=reach).astype(held_as)


def setup_inputs(seed: int = 0) -> dict:
    streams_of = jax.random.split(jax.random.key(seed), 14)
    boundary = centred(streams_of[0], (LAYERS, MICRO, TOKENS, D), 1.0, 6.0, ((0, 2), (2, 16)))
    w_query = centred(streams_of[1], (LAYERS, D, HEADS * HEAD_DIM), D ** -0.5, 0.15625, ((0, 2),))
    w_key = centred(streams_of[2], (LAYERS, D, KV_HEADS * HEAD_DIM), D ** -0.5, 0.15625, ((0, 2),))
    w_value = centred(streams_of[3], (LAYERS, D, KV_HEADS * HEAD_DIM), D ** -0.5, 0.15625, ((0, 2),))
    w_out = centred(streams_of[4], (LAYERS, HEADS * HEAD_DIM, D), (HEADS * HEAD_DIM // 16) ** -0.5, 0.625, ((0, 2),))
    norm_attn = jnp.clip(1.0 + 0.1 * jax.random.normal(streams_of[5], (LAYERS, D), jnp.float32), 0.5, 1.5)
    norm_ffn = jnp.clip(1.0 + 0.1 * jax.random.normal(streams_of[6], (LAYERS, D), jnp.float32), 0.5, 1.5)
    w_gate = centred(streams_of[7], (LAYERS, EXPERTS, D, FF), D ** -0.5, 0.15625, ((0, 2), (1, 8)))
    w_up = centred(streams_of[8], (LAYERS, EXPERTS, D, FF), D ** -0.5, 0.15625, ((0, 2), (1, 8)))
    w_down = centred(streams_of[9], (LAYERS, EXPERTS, FF, D), (FF // 4) ** -0.5, 0.4375, ((0, 2), (1, 8)))
    expert_ids_keys = jax.random.split(jax.random.fold_in(streams_of[10], 1), LAYERS * MICRO * TOKENS // TOK_MB)
    expert_ids_turns = jax.random.permutation(jax.random.fold_in(streams_of[10], 3), LAYERS * MICRO * TOKENS // TOK_MB)
    expert_ids = jax.vmap(lambda own, number: routed_block(jax.random.fold_in(streams_of[10], 2), own, number, TOK_MB, EXPERTS, TOP, CAP, 1))(expert_ids_keys, expert_ids_turns).reshape((LAYERS, MICRO, TOKENS, TOP))
    route_weights = jnp.clip(0.15 + 0.19999999 * jax.random.uniform(streams_of[11], (LAYERS, MICRO, TOKENS, TOP), jnp.float32) ** levels(streams_of[11], (LAYERS, MICRO, TOKENS, TOP), ((0, 2), (2, 16)), -0.2, 0.2), 0.15, 0.35)
    segments = draw_segments(jax.random.fold_in(streams_of[13], 71), 0)
    return dict(boundary=boundary, w_query=w_query, w_key=w_key, w_value=w_value, w_out=w_out, norm_attn=norm_attn, norm_ffn=norm_ffn, w_gate=w_gate, w_up=w_up, w_down=w_down, expert_ids=expert_ids, route_weights=route_weights, segments=segments)


EPSILON = 1e-06
HIGHEST = lax.Precision.HIGHEST

@jax.custom_vjp
def low(v):
    return lax.optimization_barrier(v.astype(jnp.bfloat16)).astype(jnp.float32)

@jax.custom_vjp
def low_back(v):
    return v

def low_keep(v):
    return (low(v), None)

def low_pass(kept, grad):
    return (grad,)

def back_keep(v):
    return (v, None)

def back_low(kept, grad):
    return (low(grad),)
low.defvjp(low_keep, low_pass)
low_back.defvjp(back_keep, back_low)

def product(matrix_a, matrix_b):
    return jnp.dot(matrix_a, matrix_b, precision=HIGHEST)

def rms_norm(values, scales):
    return values * lax.rsqrt(lax.optimization_barrier(jnp.mean(values * values, axis=-1, keepdims=True)) + EPSILON) * scales

def attend_sequence(pieces):
    queries, keys_all, values, segment = pieces
    groups = HEADS // KV_HEADS
    query_heads = queries.reshape(SEQ, KV_HEADS, groups, HEAD_DIM)
    key_heads = keys_all.reshape(SEQ, KV_HEADS, HEAD_DIM)
    value_heads = values.reshape(SEQ, KV_HEADS, HEAD_DIM)
    scores = jnp.einsum('tghd,sgd->ghts', query_heads, key_heads, precision=HIGHEST) * HEAD_DIM ** (-0.5)
    scores = low_back(scores)
    places = jnp.arange(SEQ, dtype=jnp.int32)
    allowed = (places[None, :] <= places[:, None]) & (segment[None, :] == segment[:, None])
    scores = jnp.where(allowed, scores, -1e+30)
    shifted = scores - lax.optimization_barrier(jnp.max(scores, axis=-1, keepdims=True))
    exps = jnp.exp(shifted)
    probs = low(exps / lax.optimization_barrier(jnp.sum(exps, axis=-1, keepdims=True)))
    attended = jnp.einsum('ghts,sgd->tghd', probs, value_heads, precision=HIGHEST)
    return attended.reshape(SEQ, HEADS * HEAD_DIM)

def expert_rows(pieces):
    inputs, gate_weight, up_weight, down_weight = pieces
    gate_value = low_back(product(inputs, gate_weight))
    up_value = low_back(product(inputs, up_weight))
    active = low(jax.nn.gelu(gate_value) * up_value)
    return product(active, down_weight)

def slot_index(chosen):
    blocks = TOKENS // TOK_MB
    flat_ids = chosen.reshape(blocks, TOK_MB * TOP)
    onehot = (flat_ids[:, :, None] == jnp.arange(EXPERTS, dtype=jnp.int32)[None, None, :]).astype(jnp.int32)
    within = lax.optimization_barrier(jnp.sum(jnp.cumsum(onehot, axis=1) * onehot, axis=2)) - 1
    block_base = (jnp.arange(blocks, dtype=jnp.int32) * CAP)[:, None]
    return (flat_ids * (blocks * CAP) + block_base + within).reshape(-1).astype(jnp.int32)

def layer(incoming, weights, chosen, routing, segment):
    query_weight, key_weight, value_weight, out_weight, attn_gain, ffn_gain, gate_weight, up_weight, down_weight = weights
    hidden_in = low_back(incoming)
    normed = low(rms_norm(hidden_in, attn_gain))
    queries = low_back(low(product(normed, query_weight)))
    keys_all = low_back(low(product(normed, key_weight)))
    values = low_back(low(product(normed, value_weight)))
    seq_count = TOKENS // SEQ
    attended = lax.map(jax.checkpoint(attend_sequence), (queries.reshape(seq_count, SEQ, HEADS * HEAD_DIM), keys_all.reshape(seq_count, SEQ, KV_HEADS * HEAD_DIM), values.reshape(seq_count, SEQ, KV_HEADS * HEAD_DIM), segment.reshape(seq_count, SEQ)))
    attended = low_back(low(attended.reshape(TOKENS, HEADS * HEAD_DIM)))
    branch = low_back(product(attended, out_weight))
    residual = hidden_in + branch
    normed_ffn = low(rms_norm(residual, ffn_gain))
    copies = low_back(jnp.repeat(normed_ffn, TOP, axis=0))
    slot_rows = slot_index(chosen)
    rows_all = TOKENS // TOK_MB * CAP
    buffer = jnp.zeros((EXPERTS * rows_all, D), jnp.float32).at[slot_rows].set(copies)
    outputs = lax.map(jax.checkpoint(expert_rows), (buffer.reshape(EXPERTS, rows_all, D), gate_weight, up_weight, down_weight))
    returned = low(outputs.reshape(EXPERTS * rows_all, D))[slot_rows]
    returned = low_back(returned).reshape(TOKENS, TOP, D)
    mixed_out = residual + lax.optimization_barrier(jnp.sum(routing[:, :, None] * returned, axis=1))
    return low(mixed_out)

def reference(boundary, w_query, w_key, w_value, w_out, norm_attn, norm_ffn, w_gate, w_up, w_down, expert_ids, route_weights, segments):
    weight_sets = [tuple((tensor[layer_index].astype(jnp.float32) for tensor in (w_query, w_key, w_value, w_out, norm_attn, norm_ffn, w_gate, w_up, w_down))) for layer_index in range(LAYERS)]
    grad_sets = [jax.tree.map(jnp.zeros_like, weight_sets[layer_index]) for layer_index in range(LAYERS)]
    act_rows = [[None] * MICRO for layer_index in range(LAYERS)]
    input_rows = [[None] * MICRO for layer_index in range(LAYERS)]
    for micro_index in range(MICRO):
        carried = boundary[0, micro_index].astype(jnp.float32)
        pullers = []
        for layer_index in range(LAYERS):

            def apply_layer(incoming, weights, layer_index=layer_index, micro_index=micro_index):
                return layer(incoming, weights, expert_ids[layer_index, micro_index], route_weights[layer_index, micro_index].astype(jnp.float32), segments[micro_index])
            carried, puller = jax.vjp(apply_layer, carried, weight_sets[layer_index])
            act_rows[layer_index][micro_index] = carried
            pullers.append(puller)
        cotangent = boundary[1, micro_index].astype(jnp.float32)
        for layer_index in reversed(range(LAYERS)):
            cotangent, layer_grads = pullers[layer_index](cotangent)
            input_rows[layer_index][micro_index] = cotangent
            grad_sets[layer_index] = jax.tree.map(jnp.add, grad_sets[layer_index], layer_grads)
    activations = jnp.stack([jnp.stack(act_rows[layer_index]) for layer_index in range(LAYERS)]).astype(jnp.bfloat16)
    input_grads = jnp.stack([jnp.stack(input_rows[layer_index]) for layer_index in range(LAYERS)]).astype(jnp.bfloat16)
    stacked = [jnp.stack([grad_sets[layer_index][member] for layer_index in range(LAYERS)]) for member in range(9)]
    return (activations, input_grads, stacked[0], stacked[1], stacked[2], stacked[3], stacked[4], stacked[5], stacked[6], stacked[7], stacked[8])
```

```python
import functools

import jax
import jax.numpy as jnp
from jax import lax
from jax.experimental import pallas as pl
from jax.experimental.pallas import tpu as pltpu
from jax.sharding import PartitionSpec as P

HEADS = 12
KV_HEADS = 2
HEAD_DIM = 128
GROUPS = HEADS // KV_HEADS
TOP = 4
LINE = 4
EPSILON = 1e-06
MASKED = -1e30
F32 = jnp.float32
BF16 = jnp.bfloat16
MESH = pl.DeviceIdType.MESH
VMEM_BYTES = 60 * 1024 * 1024
GELU_A = 0.7978845608028654
GELU_B = 0.044715


def dot(a, b):
    return jnp.dot(a, b, preferred_element_type=F32)


def dot_nt(a, b):
    return lax.dot_general(a, b, (((1,), (1,)), ((), ())), preferred_element_type=F32)


def dot_tn(a, b):
    return lax.dot_general(a, b, (((0,), (0,)), ((), ())), preferred_element_type=F32)


def rms_norm(values, scales):
    return values * lax.rsqrt(jnp.mean(values * values, axis=-1, keepdims=True) + EPSILON) * scales


class Sizes:
    def __init__(self, experts, micro, tokens, model, hidden):
        self.experts, self.micro, self.tokens, self.model, self.hidden = experts, micro, tokens, model, hidden
        self.line = LINE
        self.width = experts // LINE
        self.cap = 3 * tokens * TOP // (2 * experts)
        self.packed = micro * self.cap
        self.group = self.width * self.packed
        self.rows = micro * tokens


class Place:
    def __init__(self, sizes):
        self.sizes = sizes
        self.me = lax.axis_index("expert")
        self.z = self.me // sizes.width
        self.x = self.me % sizes.width

    def device(self, z, x):
        return {"expert": z * self.sizes.width + x}

    def above(self):
        return self.device(self.z + 1, self.x)

    def below(self):
        return self.device(self.z - 1, self.x)

    def peer_x(self, offset):
        return (self.x + offset) % self.sizes.width

    def near(self, step):
        z = self.z
        middle_low = jnp.where(step < 2, 1 - step, step)
        middle_high = jnp.where(step < 2, 2 + step, 3 - step)
        return jnp.where(
            z == 0, step, jnp.where(z == 3, 3 - step, jnp.where(z == 1, middle_low, middle_high))
        )

    def far(self, step):
        return self.near(self.sizes.line - 1 - step)


def remote(src, dst, send, recv, device):
    return pltpu.make_async_remote_copy(
        src_ref=src, dst_ref=dst, send_sem=send, recv_sem=recv, device_id=device, device_id_type=MESH
    )


def greet(place):
    line, width = place.sizes.line, place.sizes.width
    barrier = pltpu.get_barrier_semaphore()

    @pl.when(place.z > 0)
    def _():
        pl.semaphore_signal(barrier, inc=1, device_id=place.below(), device_id_type=MESH)

    @pl.when(place.z < line - 1)
    def _():
        pl.semaphore_signal(barrier, inc=1, device_id=place.above(), device_id_type=MESH)

    for offset in range(1, width):
        pl.semaphore_signal(
            barrier, inc=1, device_id=place.device(place.z, place.peer_x(offset)), device_id_type=MESH
        )
    count = (width - 1) + (place.z > 0).astype(jnp.int32) + (place.z < line - 1).astype(jnp.int32)
    pl.semaphore_wait(barrier, count)


def selector(ranks, cap):
    wanted = lax.broadcasted_iota(jnp.int32, (cap, ranks.shape[-1]), 0)
    return jnp.where(ranks == wanted, 1.0, 0.0).astype(BF16)


class Gather:
    def __init__(self, place, ranks, line, stage, packed, sems):
        self.place, self.ranks, self.line, self.stage, self.packed = place, ranks, line, stage, packed
        self.line_up, self.line_down, self.line_got, self.x_sent, self.x_got = sems

    def up(self, zz):
        block = self.line.at[zz]
        return remote(block, block, self.line_up.at[zz], self.line_got.at[zz], self.place.above())

    def down(self, zz):
        block = self.line.at[zz]
        return remote(block, block, self.line_down.at[zz], self.line_got.at[zz], self.place.below())

    def across(self, zz, offset):
        place = self.place
        return remote(
            self.stage.at[zz, offset - 1],
            self.packed.at[zz, place.x],
            self.x_sent.at[zz, offset - 1],
            self.x_got.at[zz, offset - 1],
            place.device(place.z, place.peer_x(offset)),
        )

    def pack(self, zz, expert_x):
        sizes = self.place.sizes
        parts = []
        for m in range(sizes.micro):
            pick = selector(self.ranks[expert_x, zz, m : m + 1, :], sizes.cap)
            parts.append(dot(pick, self.line[zz, m * sizes.tokens : (m + 1) * sizes.tokens, :]).astype(BF16))
        return parts

    def relays_up(self, zz):
        return (zz <= self.place.z) & (self.place.z < self.place.sizes.line - 1)

    def relays_down(self, zz):
        return (zz >= self.place.z) & (self.place.z > 0)

    def run(self, own, compute):
        place, sizes = self.place, self.place.sizes
        self.line[place.z] = own[...]

        def step(k, carry):
            @pl.when(k < sizes.line)
            def _():
                zz = place.near(k)

                @pl.when(zz != place.z)
                def _():
                    self.up(zz).wait_recv()

                @pl.when(self.relays_up(zz))
                def _():
                    self.up(zz).start()

                @pl.when(self.relays_down(zz))
                def _():
                    self.down(zz).start()

                for offset in range(1, sizes.width):
                    for m, part in enumerate(self.pack(zz, place.peer_x(offset))):
                        self.stage[zz, offset - 1, m * sizes.cap : (m + 1) * sizes.cap, :] = part
                    self.across(zz, offset).start()
                for m, part in enumerate(self.pack(zz, place.x)):
                    self.packed[zz, place.x, m * sizes.cap : (m + 1) * sizes.cap, :] = part

            @pl.when(k > 0)
            def _():
                zz = place.near(k - 1)
                for offset in range(1, sizes.width):
                    self.across(zz, offset).wait_recv()
                compute(zz)

            return carry

        lax.fori_loop(0, sizes.line + 1, step, 0)

        def finish(zz, carry):
            @pl.when(self.relays_up(zz))
            def _():
                self.up(zz).wait_send()

            @pl.when(self.relays_down(zz))
            def _():
                self.down(zz).wait_send()

            for offset in range(1, sizes.width):
                self.across(zz, offset).wait_send()
            return carry

        lax.fori_loop(0, sizes.line, finish, 0)


class Scatter:
    def __init__(self, place, ranks, results, crossed, up_in, down_in, chain, total, out, sems):
        self.place, self.ranks, self.results, self.crossed = place, ranks, results, crossed
        self.up_in, self.down_in, self.chain, self.total, self.out = up_in, down_in, chain, total, out
        self.x_sent, self.x_got, self.up_sent, self.up_got, self.down_sent, self.down_got = sems

    def span(self, m):
        cap = self.place.sizes.cap
        return pl.ds(m * cap, cap)

    def across(self, zz, offset, m):
        place = self.place
        return remote(
            self.results.at[zz, place.peer_x(offset), self.span(m)],
            self.crossed.at[zz, offset - 1, self.span(m)],
            self.x_sent.at[zz, offset - 1, m],
            self.x_got.at[zz, offset - 1, m],
            place.device(place.z, place.peer_x(offset)),
        )

    def up(self, zz, m):
        return remote(
            self.chain.at[zz, m], self.up_in.at[zz, m], self.up_sent.at[zz, m], self.up_got.at[zz, m],
            self.place.above(),
        )

    def down(self, zz, m):
        return remote(
            self.chain.at[zz, m], self.down_in.at[zz, m], self.down_sent.at[zz, m], self.down_got.at[zz, m],
            self.place.below(),
        )

    def run(self, side):
        place, sizes = self.place, self.place.sizes
        line, width = sizes.line, sizes.width

        def launch(k, carry):
            zz = place.far(k)
            for m in range(sizes.micro):
                for offset in range(1, width):
                    self.across(zz, offset, m).start()
            return carry

        lax.fori_loop(0, line, launch, 0)

        def step(k, carry):
            side(k)
            zz = place.far(k)
            for m in range(sizes.micro):
                pick = selector(self.ranks[place.x, zz, m : m + 1, :], sizes.cap)
                acc = dot_tn(pick, self.results[zz, place.x, m * sizes.cap : (m + 1) * sizes.cap, :])
                for offset in range(1, width):
                    sender = (place.x + width - offset) % width
                    pick = selector(self.ranks[sender, zz, m : m + 1, :], sizes.cap)
                    self.across(zz, offset, m).wait_recv()
                    acc += dot_tn(pick, self.crossed[zz, offset - 1, m * sizes.cap : (m + 1) * sizes.cap, :])
                self.total[...] = acc

                @pl.when((zz >= place.z) & (place.z > 0))
                def _():
                    self.up(zz, m).wait_recv()
                    self.total[...] += self.up_in[zz, m].astype(F32)

                @pl.when((zz <= place.z) & (place.z < line - 1))
                def _():
                    self.down(zz, m).wait_recv()
                    self.total[...] += self.down_in[zz, m].astype(F32)

                @pl.when(zz == place.z)
                def _():
                    self.out[m * sizes.tokens : (m + 1) * sizes.tokens, :] = self.total[...]

                @pl.when(zz != place.z)
                def _():
                    self.chain[zz, m] = self.total[...].astype(BF16)

                @pl.when(zz > place.z)
                def _():
                    self.up(zz, m).start()

                @pl.when(zz < place.z)
                def _():
                    self.down(zz, m).start()

            return carry

        lax.fori_loop(0, line, step, 0)

        def finish(zz, carry):
            for m in range(sizes.micro):
                for offset in range(1, width):
                    self.across(zz, offset, m).wait_send()

                @pl.when(zz > place.z)
                def _():
                    self.up(zz, m).wait_send()

                @pl.when(zz < place.z)
                def _():
                    self.down(zz, m).wait_send()

            return carry

        lax.fori_loop(0, line, finish, 0)


def gelu_parts(gate):
    inner = GELU_A * (gate + GELU_B * gate * gate * gate)
    tanh = jnp.tanh(inner)
    value = 0.5 * gate * (1.0 + tanh)
    slope = 0.5 * (1.0 + tanh) + 0.5 * gate * (1.0 - tanh * tanh) * (
        GELU_A * (1.0 + 3.0 * GELU_B * gate * gate)
    )
    return value, slope


def gather_sems(sizes):
    line, width = sizes.line, sizes.width
    dma = pltpu.SemaphoreType.DMA
    return [dma((line,)), dma((line,)), dma((line,)), dma((line, width - 1)), dma((line, width - 1))]


def scatter_sems(sizes):
    line, width, micro = sizes.line, sizes.width, sizes.micro
    dma = pltpu.SemaphoreType.DMA
    return [dma((line, width - 1, micro))] * 2 + [dma((line, micro))] * 4


def experts_forward_kernel(
    sizes, active, own, ranks, packed_weights, gate_hbm, up_hbm, down_hbm,
    out, packed_hbm, gates_hbm, ups_hbm,
    gate_w, up_w, down_w, line, stage, packed, gates, ups, acts, results, crossed, up_in, down_in, total,
    load_sems, keep_sems, *sems,
):
    @pl.when(lax.axis_index("section") == active)
    def _():
        place = Place(sizes)
        loads = [
            pltpu.make_async_copy(src, dst, load_sems.at[i])
            for i, (src, dst) in enumerate(((gate_hbm, gate_w), (up_hbm, up_w), (down_hbm, down_w)))
        ]
        for load in loads:
            load.start()
        greet(place)
        gather = Gather(place, ranks, line, stage, packed, sems[:5])
        tile = 256
        wide = 512

        def compute(zz):
            @pl.when(zz == place.z)
            def _():
                for load in loads:
                    load.wait()

            rows = packed[zz].reshape(sizes.group, sizes.model)
            for f in range(sizes.hidden // tile):
                cols = slice(f * tile, (f + 1) * tile)
                gate = dot(rows, gate_w[:, cols])
                up = dot(rows, up_w[:, cols])
                gates[zz, :, cols] = gate.astype(BF16)
                ups[zz, :, cols] = up.astype(BF16)
                value, _ = gelu_parts(gate)
                acts[:, cols] = (value * up).astype(BF16)
            weight = packed_weights[zz]
            for n in range(sizes.model // wide):
                cols = slice(n * wide, (n + 1) * wide)
                made = dot(acts[...], down_w[:, cols]) * weight
                results[zz, :, :, cols] = made.astype(BF16).reshape(sizes.width, sizes.packed, wide)

        gather.run(own, compute)
        keeps = [
            pltpu.make_async_copy(src, dst, keep_sems.at[i])
            for i, (src, dst) in enumerate(((packed, packed_hbm), (gates, gates_hbm), (ups, ups_hbm)))
        ]
        for keep in keeps:
            keep.start()
        scatter = Scatter(
            place, ranks, results, crossed, up_in, down_in,
            line.reshape(sizes.line, sizes.micro, sizes.tokens, sizes.model), total, out, sems[5:],
        )
        scatter.run(lambda k: None)
        for keep in keeps:
            keep.wait()


def vmem_spec():
    return pl.BlockSpec(memory_space=pltpu.VMEM)


def any_spec():
    return pl.BlockSpec(memory_space=pl.ANY)


def experts_forward(sizes, active, normed, ranks, packed_weights, weights):
    line, width, model, hidden = sizes.line, sizes.width, sizes.model, sizes.hidden
    shape = jax.ShapeDtypeStruct
    return pl.pallas_call(
        functools.partial(experts_forward_kernel, sizes, active),
        out_shape=(
            shape((sizes.rows, model), F32),
            shape((line, width, sizes.packed, model), BF16),
            shape((line, sizes.group, hidden), BF16),
            shape((line, sizes.group, hidden), BF16),
        ),
        in_specs=[vmem_spec()] * 3 + [any_spec()] * 3,
        out_specs=(vmem_spec(), any_spec(), any_spec(), any_spec()),
        scratch_shapes=[
            pltpu.VMEM((model, hidden), BF16),
            pltpu.VMEM((model, hidden), BF16),
            pltpu.VMEM((hidden, model), BF16),
            pltpu.VMEM((line, sizes.rows, model), BF16),
            pltpu.VMEM((line, width - 1, sizes.packed, model), BF16),
            pltpu.VMEM((line, width, sizes.packed, model), BF16),
            pltpu.VMEM((line, sizes.group, hidden), BF16),
            pltpu.VMEM((line, sizes.group, hidden), BF16),
            pltpu.VMEM((sizes.group, hidden), BF16),
            pltpu.VMEM((line, width, sizes.packed, model), BF16),
            pltpu.VMEM((line, width - 1, sizes.packed, model), BF16),
            pltpu.VMEM((line, sizes.micro, sizes.tokens, model), BF16),
            pltpu.VMEM((line, sizes.micro, sizes.tokens, model), BF16),
            pltpu.VMEM((sizes.tokens, model), F32),
            pltpu.SemaphoreType.DMA((3,)),
            pltpu.SemaphoreType.DMA((3,)),
        ]
        + gather_sems(sizes)
        + scatter_sems(sizes),
        compiler_params=pltpu.CompilerParams(
            collective_id=active, has_side_effects=True, vmem_limit_bytes=VMEM_BYTES
        ),
        name="experts_forward",
    )(normed, ranks, packed_weights, *weights)


def experts_backward_kernel(
    sizes, active, own, ranks, packed_weights, gate_hbm, up_hbm, down_hbm, packed_hbm, gates_hbm, ups_hbm,
    out, gate_grad, up_grad, down_grad,
    gate_w, up_w, down_w, line, stage, grads, packed, gates, ups, acts, results, crossed, up_in, down_in, total,
    load_sems, *sems,
):
    @pl.when(lax.axis_index("section") == active)
    def _():
        place = Place(sizes)
        pairs = (
            (down_hbm, down_w), (gates_hbm, gates), (ups_hbm, ups),
            (gate_hbm, gate_w), (up_hbm, up_w), (packed_hbm, packed),
        )
        loads = [pltpu.make_async_copy(src, dst, load_sems.at[i]) for i, (src, dst) in enumerate(pairs)]
        for load in loads:
            load.start()
        greet(place)
        gather = Gather(place, ranks, line, stage, grads, sems[:5])
        tile = 256
        wide = 512

        def compute(zz):
            @pl.when(zz == place.z)
            def _():
                for load in loads:
                    load.wait()

            rows = grads[zz].reshape(sizes.group, sizes.model)
            weight = packed_weights[zz]
            for f in range(sizes.hidden // tile):
                cols = slice(f * tile, (f + 1) * tile)
                act_grad = dot_nt(rows, down_w[cols, :]) * weight
                up = ups[zz, :, cols].astype(F32)
                value, slope = gelu_parts(gates[zz, :, cols].astype(F32))
                acts[zz, :, cols] = (value * up * weight).astype(BF16)
                gates[zz, :, cols] = (act_grad * up * slope).astype(BF16)
                ups[zz, :, cols] = (act_grad * value).astype(BF16)
            for n in range(sizes.model // wide):
                cols = slice(n * wide, (n + 1) * wide)
                made = dot_nt(gates[zz], gate_w[cols, :]) + dot_nt(ups[zz], up_w[cols, :])
                results[zz, :, :, cols] = made.astype(BF16).reshape(sizes.width, sizes.packed, wide)

        gather.run(own, compute)
        scatter = Scatter(
            place, ranks, results, crossed, up_in, down_in,
            line.reshape(sizes.line, sizes.micro, sizes.tokens, sizes.model), total, out, sems[5:],
        )
        total_rows = sizes.line * sizes.group
        part = sizes.model // sizes.line

        def weight_grads(k):
            cols = pl.ds(pl.multiple_of(k * part, 128), part)
            rows = packed[:, :, :, cols].reshape(total_rows, part)
            gate_grad[cols, :] = dot_tn(rows, gates[...].reshape(total_rows, sizes.hidden)).astype(BF16)
            up_grad[cols, :] = dot_tn(rows, ups[...].reshape(total_rows, sizes.hidden)).astype(BF16)
            down_grad[:, cols] = dot_tn(
                acts[...].reshape(total_rows, sizes.hidden), grads[:, :, :, cols].reshape(total_rows, part)
            ).astype(BF16)

        scatter.run(weight_grads)


def experts_backward(sizes, active, upstream, ranks, packed_weights, weights, kept):
    line, width, model, hidden = sizes.line, sizes.width, sizes.model, sizes.hidden
    shape = jax.ShapeDtypeStruct
    return pl.pallas_call(
        functools.partial(experts_backward_kernel, sizes, active),
        out_shape=(
            shape((sizes.rows, model), F32),
            shape((model, hidden), BF16),
            shape((model, hidden), BF16),
            shape((hidden, model), BF16),
        ),
        in_specs=[vmem_spec()] * 3 + [any_spec()] * 6,
        out_specs=(vmem_spec(),) * 4,
        scratch_shapes=[
            pltpu.VMEM((model, hidden), BF16),
            pltpu.VMEM((model, hidden), BF16),
            pltpu.VMEM((hidden, model), BF16),
            pltpu.VMEM((line, sizes.rows, model), BF16),
            pltpu.VMEM((line, width - 1, sizes.packed, model), BF16),
            pltpu.VMEM((line, width, sizes.packed, model), BF16),
            pltpu.VMEM((line, width, sizes.packed, model), BF16),
            pltpu.VMEM((line, sizes.group, hidden), BF16),
            pltpu.VMEM((line, sizes.group, hidden), BF16),
            pltpu.VMEM((line, sizes.group, hidden), BF16),
            pltpu.VMEM((line, width, sizes.packed, model), BF16),
            pltpu.VMEM((line, width - 1, sizes.packed, model), BF16),
            pltpu.VMEM((line, sizes.micro, sizes.tokens, model), BF16),
            pltpu.VMEM((line, sizes.micro, sizes.tokens, model), BF16),
            pltpu.VMEM((sizes.tokens, model), F32),
            pltpu.SemaphoreType.DMA((6,)),
        ]
        + gather_sems(sizes)
        + scatter_sems(sizes),
        compiler_params=pltpu.CompilerParams(
            collective_id=2 + active, has_side_effects=True, vmem_limit_bytes=VMEM_BYTES
        ),
        name="experts_backward",
    )(upstream, ranks, packed_weights, *weights, *kept)


def routing_tables(sizes, expert_ids, route_weights):
    experts, cap = sizes.experts, sizes.cap
    me = lax.axis_index("expert")
    z, x = me // sizes.width, me % sizes.width
    named = expert_ids[:, None, :, :] == jnp.arange(experts, dtype=jnp.int32)[None, :, None, None]
    used = jnp.any(named, axis=-1)
    weight = jnp.sum(jnp.where(named, route_weights[:, None, :, :], 0.0), axis=-1)
    before = jnp.triu(jnp.ones((sizes.tokens, sizes.tokens), BF16), 1)
    rank = jnp.where(used, dot(used.astype(BF16), before), -1.0)
    both = lax.all_gather(jnp.stack([rank, weight]), "expert", axis=0, tiled=False)
    both = both.reshape(sizes.line, sizes.width, 2, sizes.micro, experts, sizes.tokens)
    here = lax.dynamic_index_in_dim(both[:, :, 0], x, 1, keepdims=False)
    here = lax.dynamic_slice_in_dim(here, z * sizes.width, sizes.width, axis=2)
    ranks = jnp.transpose(here, (2, 0, 1, 3)).astype(jnp.int32)
    mine = lax.dynamic_index_in_dim(both, me, 4, keepdims=False)
    slots = jnp.arange(cap, dtype=F32)
    hit = mine[:, :, 0, :, None, :] == slots[None, None, None, :, None]
    packed = jnp.sum(jnp.where(hit, mine[:, :, 1, :, None, :], 0.0), axis=-1)
    return ranks, packed.reshape(sizes.line, sizes.group, 1)


def masked_scores(query_heads, key_heads, allowed):
    scaled = jnp.einsum("mtghd,msgd->mghts", query_heads, key_heads, preferred_element_type=F32)
    return jnp.where(allowed[:, None, None], scaled * HEAD_DIM ** (-0.5), MASKED)


def gather_sequence(value):
    both = lax.all_gather(value, "dp", axis=1, tiled=True)
    return both


def attention_forward(incoming, params, allowed):
    micro, tokens, model = incoming.shape
    query_w, key_w, value_w, out_w, attn_gain, ffn_gain = params
    hidden_in = incoming.astype(F32).reshape(micro * tokens, model)
    normed = rms_norm(hidden_in, attn_gain).astype(BF16)
    queries = dot(normed, query_w).astype(BF16)
    own_kv = jnp.concatenate([dot(normed, key_w).astype(BF16), dot(normed, value_w).astype(BF16)], axis=1)
    both = gather_sequence(own_kv.reshape(micro, tokens, -1))
    seq = both.shape[1]
    both = both.reshape(micro, seq, 2, KV_HEADS, HEAD_DIM)
    key_heads, value_heads = both[:, :, 0], both[:, :, 1]
    query_heads = queries.reshape(micro, tokens, KV_HEADS, GROUPS, HEAD_DIM)
    scores = masked_scores(query_heads, key_heads, allowed)
    peak = jnp.max(scores, axis=-1, keepdims=True)
    log_total = peak + jnp.log(jnp.sum(jnp.exp(scores - peak), axis=-1, keepdims=True))
    probs = jnp.exp(scores - log_total).astype(BF16)
    attended = jnp.einsum("mghts,msgd->mtghd", probs, value_heads, preferred_element_type=F32)
    attended = attended.reshape(micro * tokens, HEADS * HEAD_DIM).astype(BF16)
    residual = hidden_in + dot(attended, out_w)
    normed_ffn = rms_norm(residual, ffn_gain).astype(BF16)
    return normed_ffn, (hidden_in, normed, query_heads, key_heads, value_heads, log_total, attended, residual)


def attention_backward(upstream, ffn_in_grad, stored, params, allowed):
    query_w, key_w, value_w, out_w, attn_gain, ffn_gain = params
    hidden_in, normed, query_heads, key_heads, value_heads, log_total, attended, residual = stored
    micro, tokens = query_heads.shape[:2]
    seq = key_heads.shape[1]
    rows = micro * tokens
    _, pull_ffn = jax.vjp(rms_norm, residual, ffn_gain)
    residual_part, ffn_gain_grad = pull_ffn(ffn_in_grad)
    residual_grad = upstream.astype(F32) + residual_part
    branch_grad = residual_grad.astype(BF16)
    out_grad = dot_tn(attended, branch_grad)
    attended_grad = dot_nt(branch_grad, out_w).astype(BF16)
    scores = masked_scores(query_heads, key_heads, allowed)
    probs_full = jnp.exp(scores - log_total)
    probs_low = probs_full.astype(BF16)
    grad_heads = attended_grad.reshape(micro, tokens, KV_HEADS, GROUPS, HEAD_DIM)
    value_part = jnp.einsum("mghts,mtghd->msgd", probs_low, grad_heads, preferred_element_type=F32)
    probs_grad = jnp.einsum("mtghd,msgd->mghts", grad_heads, value_heads, preferred_element_type=F32)
    score_grad = probs_full * (probs_grad - jnp.sum(probs_grad * probs_full, axis=-1, keepdims=True))
    score_grad = score_grad.astype(BF16)
    scale = HEAD_DIM ** (-0.5)
    query_grad = jnp.einsum("mghts,msgd->mtghd", score_grad, key_heads, preferred_element_type=F32) * scale
    query_grad = query_grad.reshape(rows, HEADS * HEAD_DIM).astype(BF16)
    key_part = jnp.einsum("mghts,mtghd->msgd", score_grad, query_heads, preferred_element_type=F32) * scale
    kv_width = KV_HEADS * HEAD_DIM
    kv_part = jnp.concatenate(
        [key_part.reshape(micro, seq, kv_width), value_part.reshape(micro, seq, kv_width)], axis=2
    ).astype(BF16)
    kv_grad = lax.psum_scatter(kv_part, "dp", scatter_dimension=1, tiled=True)
    kv_grad = kv_grad.reshape(rows, 2 * kv_width)
    key_grad, value_grad = kv_grad[:, :kv_width], kv_grad[:, kv_width:]
    normed_grad = dot_nt(query_grad, query_w) + dot_nt(key_grad, key_w) + dot_nt(value_grad, value_w)
    _, pull_attn = jax.vjp(rms_norm, hidden_in, attn_gain)
    hidden_part, attn_gain_grad = pull_attn(normed_grad)
    incoming_grad = (residual_grad + hidden_part).astype(BF16)
    grads = (
        dot_tn(normed, query_grad).astype(BF16),
        dot_tn(normed, kv_grad).astype(BF16),
        out_grad.astype(BF16),
        attn_gain_grad,
        ffn_gain_grad,
    )
    return incoming_grad, grads


def per_device(
    boundary, w_query, w_key, w_value, w_out, norm_attn, norm_ffn, w_gate, w_up, w_down,
    expert_ids, route_weights, segments,
):
    micro, tokens, model = boundary.shape[1:]
    sizes = Sizes(lax.axis_size("expert"), micro, tokens, model, w_gate.shape[-1])
    first = lax.axis_index("section") == 0
    offset = lax.axis_index("dp") * tokens
    seq = segments.shape[1]
    params = (w_query[0], w_key[0], w_value[0], w_out[0], norm_attn[0], norm_ffn[0])
    expert_params = (w_gate[0, 0], w_up[0, 0], w_down[0, 0])
    ranks, packed_weights = routing_tables(sizes, expert_ids[0], route_weights[0])
    query_pos = offset + jnp.arange(tokens, dtype=jnp.int32)
    query_seg = lax.dynamic_slice_in_dim(segments, offset, tokens, axis=1)
    allowed = (jnp.arange(seq, dtype=jnp.int32)[None, :] <= query_pos[:, None])[None] & (
        segments[:, None, :] == query_seg[:, :, None]
    )

    def forward(step, incoming):
        normed_ffn, stored = attention_forward(incoming, params, allowed)
        mixed, *kept = experts_forward(sizes, step, normed_ffn, ranks, packed_weights, expert_params)
        return (stored[-1] + mixed).astype(BF16), stored, kept

    def backward(step, upstream, stored, kept):
        ffn_in_grad, *expert_grads = experts_backward(
            sizes, step, upstream, ranks, packed_weights, expert_params, kept
        )
        incoming_grad, grads = attention_backward(upstream, ffn_in_grad, stored, params, allowed)
        return incoming_grad, grads, expert_grads

    out_0, stored_0, kept_0 = forward(0, boundary[0])
    received = lax.ppermute(out_0, "section", [(0, 1)]).reshape(micro, tokens, model)
    out_1, stored_1, kept_1 = forward(1, received)
    upstream_1 = boundary[0].reshape(sizes.rows, model)
    in_grad_1, grads_1, expert_grads_1 = backward(1, upstream_1, stored_1, kept_1)
    upstream_0 = lax.ppermute(in_grad_1, "section", [(1, 0)])
    in_grad_0, grads_0, expert_grads_0 = backward(0, upstream_0, stored_0, kept_0)

    def choose(a, b):
        return jnp.where(first, a, b)

    activations = choose(out_0, out_1).reshape(1, micro, tokens, model)
    input_grads = choose(in_grad_0, in_grad_1).reshape(1, micro, tokens, model)
    dense = [choose(a, b) for a, b in zip(grads_0, grads_1)]
    experts = [choose(a, b) for a, b in zip(expert_grads_0, expert_grads_1)]
    sums = lax.psum(tuple(dense[:3]), ("expert", "dp"))
    gains = lax.psum(jnp.stack(dense[3:]), ("expert", "dp"))
    expert_sums = [
        lax.psum_scatter(experts[0], "dp", scatter_dimension=0, tiled=True),
        lax.psum_scatter(experts[1], "dp", scatter_dimension=0, tiled=True),
        lax.psum_scatter(experts[2], "dp", scatter_dimension=1, tiled=True),
    ]
    kv_width = KV_HEADS * HEAD_DIM
    return (
        activations,
        input_grads,
        sums[0].astype(F32)[None],
        sums[1][:, :kv_width].astype(F32)[None],
        sums[1][:, kv_width:].astype(F32)[None],
        sums[2].astype(F32)[None],
        gains[0][None],
        gains[1][None],
        expert_sums[0].astype(F32)[None, None],
        expert_sums[1].astype(F32)[None, None],
        expert_sums[2].astype(F32)[None, None],
    )


def solution(mesh):
    in_specs = (
        P("section", None, ("expert", "dp"), None),
        P("section", None, None),
        P("section", None, None),
        P("section", None, None),
        P("section", None, None),
        P("section", None),
        P("section", None),
        P("section", "expert", None, None),
        P("section", "expert", None, None),
        P("section", "expert", None, None),
        P("section", None, ("expert", "dp"), None),
        P("section", None, ("expert", "dp"), None),
        P(None, "expert"),
    )
    out_specs = (
        P("section", None, ("expert", "dp"), None),
        P("section", None, ("expert", "dp"), None),
        P("section", None, None),
        P("section", None, None),
        P("section", None, None),
        P("section", None, None),
        P("section", None),
        P("section", None),
        P("section", "expert", "dp", None),
        P("section", "expert", "dp", None),
        P("section", "expert", None, "dp"),
    )
    return jax.shard_map(
        per_device, mesh=mesh, in_specs=in_specs, out_specs=out_specs, check_vma=False
    )
```

```python
import functools

import jax
import jax.numpy as jnp
from jax import lax
from jax.experimental import pallas as pl
from jax.experimental.pallas import tpu as pltpu
from jax.sharding import PartitionSpec as P

HEADS = 12
KV_HEADS = 2
HEAD_DIM = 128
GROUPS = HEADS // KV_HEADS
TOP = 4
LINE = 4
EPSILON = 1e-06
MASKED = -1e30
F32 = jnp.float32
BF16 = jnp.bfloat16
MESH = pl.DeviceIdType.MESH
VMEM_BYTES = 60 * 1024 * 1024
GELU_A = 0.7978845608028654
GELU_B = 0.044715


def dot(a, b):
    return jnp.dot(a, b, preferred_element_type=F32)


def dot_nt(a, b):
    return lax.dot_general(a, b, (((1,), (1,)), ((), ())), preferred_element_type=F32)


def dot_tn(a, b):
    return lax.dot_general(a, b, (((0,), (0,)), ((), ())), preferred_element_type=F32)


def rms_norm(values, scales):
    return values * lax.rsqrt(jnp.mean(values * values, axis=-1, keepdims=True) + EPSILON) * scales


class Sizes:
    def __init__(self, experts, copies, micro, tokens, model, hidden):
        self.experts, self.copies, self.micro, self.tokens = experts, copies, micro, tokens
        self.model, self.hidden = model, hidden
        self.seq = copies * tokens
        self.line = LINE
        self.width = experts // LINE
        self.cap = 3 * tokens * TOP // (2 * experts)
        self.packed = micro * self.cap
        self.group = self.width * self.packed
        self.rows = micro * tokens


class Place:
    def __init__(self, sizes):
        self.sizes = sizes
        self.me = lax.axis_index("expert")
        self.z = self.me // sizes.width
        self.x = self.me % sizes.width

    def device(self, z, x):
        return {"expert": z * self.sizes.width + x}

    def above(self):
        return self.device(self.z + 1, self.x)

    def below(self):
        return self.device(self.z - 1, self.x)

    def peer_x(self, offset):
        return (self.x + offset) % self.sizes.width

    def near(self, step):
        z = self.z
        middle_low = jnp.where(step < 2, 1 - step, step)
        middle_high = jnp.where(step < 2, 2 + step, 3 - step)
        return jnp.where(
            z == 0, step, jnp.where(z == 3, 3 - step, jnp.where(z == 1, middle_low, middle_high))
        )

    def far(self, step):
        return self.near(self.sizes.line - 1 - step)


def remote(src, dst, send, recv, device):
    return pltpu.make_async_remote_copy(
        src_ref=src, dst_ref=dst, send_sem=send, recv_sem=recv, device_id=device, device_id_type=MESH
    )


def greet(place):
    line, width = place.sizes.line, place.sizes.width
    barrier = pltpu.get_barrier_semaphore()

    @pl.when(place.z > 0)
    def _():
        pl.semaphore_signal(barrier, inc=1, device_id=place.below(), device_id_type=MESH)

    @pl.when(place.z < line - 1)
    def _():
        pl.semaphore_signal(barrier, inc=1, device_id=place.above(), device_id_type=MESH)

    for offset in range(1, width):
        pl.semaphore_signal(
            barrier, inc=1, device_id=place.device(place.z, place.peer_x(offset)), device_id_type=MESH
        )
    count = (width - 1) + (place.z > 0).astype(jnp.int32) + (place.z < line - 1).astype(jnp.int32)
    pl.semaphore_wait(barrier, count)


class Routing:
    def __init__(self, place, table):
        self.place, self.table = place, table

    def hits(self, zz, xx, expert_x, m):
        sizes = self.place.sizes
        rows = self.table[zz, xx, self.place.z * sizes.width + expert_x]
        wanted = lax.broadcasted_iota(jnp.int32, (sizes.cap, sizes.tokens), 0).astype(F32)
        return rows[m : m + 1] == wanted, rows[sizes.micro + m : sizes.micro + m + 1]

    def selector(self, zz, expert_x, m):
        hit, _ = self.hits(zz, self.place.x, expert_x, m)
        return jnp.where(hit, 1.0, 0.0).astype(BF16)

    def weights(self, zz):
        sizes = self.place.sizes
        parts = []
        for xx in range(sizes.width):
            for m in range(sizes.micro):
                hit, weight = self.hits(zz, xx, self.place.x, m)
                parts.append(jnp.sum(jnp.where(hit, weight, 0.0), axis=1, keepdims=True))
        return jnp.concatenate(parts, axis=0)


class Gather:
    def __init__(self, place, routing, line, stage, packed, sems):
        self.place, self.routing, self.line, self.stage, self.packed = place, routing, line, stage, packed
        self.line_up, self.line_down, self.line_got, self.x_sent, self.x_got = sems

    def up(self, zz):
        block = self.line.at[zz]
        return remote(block, block, self.line_up.at[zz], self.line_got.at[zz], self.place.above())

    def down(self, zz):
        block = self.line.at[zz]
        return remote(block, block, self.line_down.at[zz], self.line_got.at[zz], self.place.below())

    def across(self, zz, offset):
        place = self.place
        return remote(
            self.stage.at[zz, offset - 1],
            self.packed.at[zz, place.x],
            self.x_sent.at[zz, offset - 1],
            self.x_got.at[zz, offset - 1],
            place.device(place.z, place.peer_x(offset)),
        )

    def pack(self, zz, expert_x):
        sizes = self.place.sizes
        parts = []
        for m in range(sizes.micro):
            pick = self.routing.selector(zz, expert_x, m)
            parts.append(dot(pick, self.line[zz, m * sizes.tokens : (m + 1) * sizes.tokens, :]).astype(BF16))
        return parts

    def relays_up(self, zz):
        return (zz <= self.place.z) & (self.place.z < self.place.sizes.line - 1)

    def relays_down(self, zz):
        return (zz >= self.place.z) & (self.place.z > 0)

    def run(self, own, compute):
        place, sizes = self.place, self.place.sizes
        self.line[place.z] = own[...]

        def step(k, carry):
            @pl.when(k < sizes.line)
            def _():
                zz = place.near(k)

                @pl.when(zz != place.z)
                def _():
                    self.up(zz).wait_recv()

                @pl.when(self.relays_up(zz))
                def _():
                    self.up(zz).start()

                @pl.when(self.relays_down(zz))
                def _():
                    self.down(zz).start()

                for offset in range(1, sizes.width):
                    for m, part in enumerate(self.pack(zz, place.peer_x(offset))):
                        self.stage[zz, offset - 1, m * sizes.cap : (m + 1) * sizes.cap, :] = part
                    self.across(zz, offset).start()
                for m, part in enumerate(self.pack(zz, place.x)):
                    self.packed[zz, place.x, m * sizes.cap : (m + 1) * sizes.cap, :] = part

            @pl.when(k > 0)
            def _():
                zz = place.near(k - 1)
                for offset in range(1, sizes.width):
                    self.across(zz, offset).wait_recv()
                compute(zz)

            return carry

        lax.fori_loop(0, sizes.line + 1, step, 0)

        def finish(zz, carry):
            @pl.when(self.relays_up(zz))
            def _():
                self.up(zz).wait_send()

            @pl.when(self.relays_down(zz))
            def _():
                self.down(zz).wait_send()

            for offset in range(1, sizes.width):
                self.across(zz, offset).wait_send()
            return carry

        lax.fori_loop(0, sizes.line, finish, 0)


class Scatter:
    def __init__(self, place, routing, results, crossed, up_in, down_in, chain, total, out, sems):
        self.place, self.routing, self.results, self.crossed = place, routing, results, crossed
        self.up_in, self.down_in, self.chain, self.total, self.out = up_in, down_in, chain, total, out
        self.x_sent, self.x_got, self.up_sent, self.up_got, self.down_sent, self.down_got = sems

    def span(self, m):
        cap = self.place.sizes.cap
        return pl.ds(m * cap, cap)

    def across(self, zz, offset, m):
        place = self.place
        return remote(
            self.results.at[zz, place.peer_x(offset), self.span(m)],
            self.crossed.at[zz, offset - 1, self.span(m)],
            self.x_sent.at[zz, offset - 1, m],
            self.x_got.at[zz, offset - 1, m],
            place.device(place.z, place.peer_x(offset)),
        )

    def up(self, zz, m):
        return remote(
            self.chain.at[zz, m], self.up_in.at[zz, m], self.up_sent.at[zz, m], self.up_got.at[zz, m],
            self.place.above(),
        )

    def down(self, zz, m):
        return remote(
            self.chain.at[zz, m], self.down_in.at[zz, m], self.down_sent.at[zz, m], self.down_got.at[zz, m],
            self.place.below(),
        )

    def run(self, side):
        place, sizes = self.place, self.place.sizes
        line, width = sizes.line, sizes.width

        def launch(k, carry):
            zz = place.far(k)
            for m in range(sizes.micro):
                for offset in range(1, width):
                    self.across(zz, offset, m).start()
            return carry

        lax.fori_loop(0, line, launch, 0)

        def step(k, carry):
            side(k)
            zz = place.far(k)
            for m in range(sizes.micro):
                pick = self.routing.selector(zz, place.x, m)
                acc = dot_tn(pick, self.results[zz, place.x, m * sizes.cap : (m + 1) * sizes.cap, :])
                for offset in range(1, width):
                    sender = (place.x + width - offset) % width
                    pick = self.routing.selector(zz, sender, m)
                    self.across(zz, offset, m).wait_recv()
                    acc += dot_tn(pick, self.crossed[zz, offset - 1, m * sizes.cap : (m + 1) * sizes.cap, :])
                self.total[...] = acc

                @pl.when((zz >= place.z) & (place.z > 0))
                def _():
                    self.up(zz, m).wait_recv()
                    self.total[...] += self.up_in[zz, m].astype(F32)

                @pl.when((zz <= place.z) & (place.z < line - 1))
                def _():
                    self.down(zz, m).wait_recv()
                    self.total[...] += self.down_in[zz, m].astype(F32)

                @pl.when(zz == place.z)
                def _():
                    self.out[m * sizes.tokens : (m + 1) * sizes.tokens, :] = self.total[...]

                @pl.when(zz != place.z)
                def _():
                    self.chain[zz, m] = self.total[...].astype(BF16)

                @pl.when(zz > place.z)
                def _():
                    self.up(zz, m).start()

                @pl.when(zz < place.z)
                def _():
                    self.down(zz, m).start()

            return carry

        lax.fori_loop(0, line, step, 0)

        def finish(zz, carry):
            for m in range(sizes.micro):
                for offset in range(1, width):
                    self.across(zz, offset, m).wait_send()

                @pl.when(zz > place.z)
                def _():
                    self.up(zz, m).wait_send()

                @pl.when(zz < place.z)
                def _():
                    self.down(zz, m).wait_send()

            return carry

        lax.fori_loop(0, line, finish, 0)


def gelu_parts(gate):
    inner = GELU_A * (gate + GELU_B * gate * gate * gate)
    tanh = jnp.tanh(inner)
    value = 0.5 * gate * (1.0 + tanh)
    slope = 0.5 * (1.0 + tanh) + 0.5 * gate * (1.0 - tanh * tanh) * (
        GELU_A * (1.0 + 3.0 * GELU_B * gate * gate)
    )
    return value, slope


def gather_sems(sizes):
    line, width = sizes.line, sizes.width
    dma = pltpu.SemaphoreType.DMA
    return [dma((line,)), dma((line,)), dma((line,)), dma((line, width - 1)), dma((line, width - 1))]


def scatter_sems(sizes):
    line, width, micro = sizes.line, sizes.width, sizes.micro
    dma = pltpu.SemaphoreType.DMA
    return [dma((line, width - 1, micro))] * 2 + [dma((line, micro))] * 4


def experts_forward_kernel(
    sizes, active, own, table, gate_hbm, up_hbm, down_hbm,
    out, packed_hbm, gates_hbm, ups_hbm,
    gate_w, up_w, down_w, line, stage, packed, gates, ups, acts, results, crossed, up_in, down_in, total,
    load_sems, keep_sems, *sems,
):
    @pl.when(lax.axis_index("section") == active)
    def _():
        place = Place(sizes)
        loads = [
            pltpu.make_async_copy(src, dst, load_sems.at[i])
            for i, (src, dst) in enumerate(((gate_hbm, gate_w), (up_hbm, up_w), (down_hbm, down_w)))
        ]
        for load in loads:
            load.start()
        greet(place)
        routing = Routing(place, table)
        gather = Gather(place, routing, line, stage, packed, sems[:5])
        tile = 256
        wide = 512

        def compute(zz):
            @pl.when(zz == place.z)
            def _():
                for load in loads:
                    load.wait()

            rows = packed[zz].reshape(sizes.group, sizes.model)
            for f in range(sizes.hidden // tile):
                cols = slice(f * tile, (f + 1) * tile)
                gate = dot(rows, gate_w[:, cols])
                up = dot(rows, up_w[:, cols])
                gates[zz, :, cols] = gate.astype(BF16)
                ups[zz, :, cols] = up.astype(BF16)
                value, _ = gelu_parts(gate)
                acts[:, cols] = (value * up).astype(BF16)
            weight = routing.weights(zz)
            for n in range(sizes.model // wide):
                cols = slice(n * wide, (n + 1) * wide)
                made = dot(acts[...], down_w[:, cols]) * weight
                results[zz, :, :, cols] = made.astype(BF16).reshape(sizes.width, sizes.packed, wide)

        gather.run(own, compute)
        keeps = [
            pltpu.make_async_copy(src, dst, keep_sems.at[i])
            for i, (src, dst) in enumerate(((packed, packed_hbm), (gates, gates_hbm), (ups, ups_hbm)))
        ]
        for keep in keeps:
            keep.start()
        scatter = Scatter(
            place, routing, results, crossed, up_in, down_in,
            line.reshape(sizes.line, sizes.micro, sizes.tokens, sizes.model), total, out, sems[5:],
        )
        scatter.run(lambda k: None)
        for keep in keeps:
            keep.wait()


def vmem_spec():
    return pl.BlockSpec(memory_space=pltpu.VMEM)


def any_spec():
    return pl.BlockSpec(memory_space=pl.ANY)


def experts_forward(sizes, active, normed, table, weights):
    line, width, model, hidden = sizes.line, sizes.width, sizes.model, sizes.hidden
    shape = jax.ShapeDtypeStruct
    return pl.pallas_call(
        functools.partial(experts_forward_kernel, sizes, active),
        out_shape=(
            shape((sizes.rows, model), F32),
            shape((line, width, sizes.packed, model), BF16),
            shape((line, sizes.group, hidden), BF16),
            shape((line, sizes.group, hidden), BF16),
        ),
        in_specs=[vmem_spec()] * 2 + [any_spec()] * 3,
        out_specs=(vmem_spec(), any_spec(), any_spec(), any_spec()),
        scratch_shapes=[
            pltpu.VMEM((model, hidden), BF16),
            pltpu.VMEM((model, hidden), BF16),
            pltpu.VMEM((hidden, model), BF16),
            pltpu.VMEM((line, sizes.rows, model), BF16),
            pltpu.VMEM((line, width - 1, sizes.packed, model), BF16),
            pltpu.VMEM((line, width, sizes.packed, model), BF16),
            pltpu.VMEM((line, sizes.group, hidden), BF16),
            pltpu.VMEM((line, sizes.group, hidden), BF16),
            pltpu.VMEM((sizes.group, hidden), BF16),
            pltpu.VMEM((line, width, sizes.packed, model), BF16),
            pltpu.VMEM((line, width - 1, sizes.packed, model), BF16),
            pltpu.VMEM((line, sizes.micro, sizes.tokens, model), BF16),
            pltpu.VMEM((line, sizes.micro, sizes.tokens, model), BF16),
            pltpu.VMEM((sizes.tokens, model), F32),
            pltpu.SemaphoreType.DMA((3,)),
            pltpu.SemaphoreType.DMA((3,)),
        ]
        + gather_sems(sizes)
        + scatter_sems(sizes),
        compiler_params=pltpu.CompilerParams(
            collective_id=active, has_side_effects=True, vmem_limit_bytes=VMEM_BYTES
        ),
        name="experts_forward",
    )(normed, table, *weights)


def experts_backward_kernel(
    sizes, active, own, table, gate_hbm, up_hbm, down_hbm, packed_hbm, gates_hbm, ups_hbm,
    out, gate_grad, up_grad, down_grad,
    gate_w, up_w, down_w, line, stage, grads, packed, gates, ups, acts, results, crossed, up_in, down_in, total,
    load_sems, *sems,
):
    @pl.when(lax.axis_index("section") == active)
    def _():
        place = Place(sizes)
        pairs = (
            (down_hbm, down_w), (gates_hbm, gates), (ups_hbm, ups),
            (gate_hbm, gate_w), (up_hbm, up_w), (packed_hbm, packed),
        )
        loads = [pltpu.make_async_copy(src, dst, load_sems.at[i]) for i, (src, dst) in enumerate(pairs)]
        for load in loads:
            load.start()
        greet(place)
        routing = Routing(place, table)
        gather = Gather(place, routing, line, stage, grads, sems[:5])
        tile = 256
        wide = 512

        def compute(zz):
            @pl.when(zz == place.z)
            def _():
                for load in loads:
                    load.wait()

            rows = grads[zz].reshape(sizes.group, sizes.model)
            weight = routing.weights(zz)
            for f in range(sizes.hidden // tile):
                cols = slice(f * tile, (f + 1) * tile)
                act_grad = dot_nt(rows, down_w[cols, :]) * weight
                up = ups[zz, :, cols].astype(F32)
                value, slope = gelu_parts(gates[zz, :, cols].astype(F32))
                acts[zz, :, cols] = (value * up * weight).astype(BF16)
                gates[zz, :, cols] = (act_grad * up * slope).astype(BF16)
                ups[zz, :, cols] = (act_grad * value).astype(BF16)
            for n in range(sizes.model // wide):
                cols = slice(n * wide, (n + 1) * wide)
                made = dot_nt(gates[zz], gate_w[cols, :]) + dot_nt(ups[zz], up_w[cols, :])
                results[zz, :, :, cols] = made.astype(BF16).reshape(sizes.width, sizes.packed, wide)

        gather.run(own, compute)
        scatter = Scatter(
            place, routing, results, crossed, up_in, down_in,
            line.reshape(sizes.line, sizes.micro, sizes.tokens, sizes.model), total, out, sems[5:],
        )
        total_rows = sizes.line * sizes.group
        part = sizes.model // sizes.line

        def weight_grads(k):
            cols = pl.ds(pl.multiple_of(k * part, 128), part)
            rows = packed[:, :, :, cols].reshape(total_rows, part)
            gate_grad[cols, :] = dot_tn(rows, gates[...].reshape(total_rows, sizes.hidden)).astype(BF16)
            up_grad[cols, :] = dot_tn(rows, ups[...].reshape(total_rows, sizes.hidden)).astype(BF16)
            down_grad[:, cols] = dot_tn(
                acts[...].reshape(total_rows, sizes.hidden), grads[:, :, :, cols].reshape(total_rows, part)
            ).astype(BF16)

        scatter.run(weight_grads)


def experts_backward(sizes, active, upstream, table, weights, kept):
    line, width, model, hidden = sizes.line, sizes.width, sizes.model, sizes.hidden
    shape = jax.ShapeDtypeStruct
    return pl.pallas_call(
        functools.partial(experts_backward_kernel, sizes, active),
        out_shape=(
            shape((sizes.rows, model), F32),
            shape((model, hidden), BF16),
            shape((model, hidden), BF16),
            shape((hidden, model), BF16),
        ),
        in_specs=[vmem_spec()] * 2 + [any_spec()] * 6,
        out_specs=(vmem_spec(),) * 4,
        scratch_shapes=[
            pltpu.VMEM((model, hidden), BF16),
            pltpu.VMEM((model, hidden), BF16),
            pltpu.VMEM((hidden, model), BF16),
            pltpu.VMEM((line, sizes.rows, model), BF16),
            pltpu.VMEM((line, width - 1, sizes.packed, model), BF16),
            pltpu.VMEM((line, width, sizes.packed, model), BF16),
            pltpu.VMEM((line, width, sizes.packed, model), BF16),
            pltpu.VMEM((line, sizes.group, hidden), BF16),
            pltpu.VMEM((line, sizes.group, hidden), BF16),
            pltpu.VMEM((line, sizes.group, hidden), BF16),
            pltpu.VMEM((line, width, sizes.packed, model), BF16),
            pltpu.VMEM((line, width - 1, sizes.packed, model), BF16),
            pltpu.VMEM((line, sizes.micro, sizes.tokens, model), BF16),
            pltpu.VMEM((line, sizes.micro, sizes.tokens, model), BF16),
            pltpu.VMEM((sizes.tokens, model), F32),
            pltpu.SemaphoreType.DMA((6,)),
        ]
        + gather_sems(sizes)
        + scatter_sems(sizes),
        compiler_params=pltpu.CompilerParams(
            collective_id=2 + active, has_side_effects=True, vmem_limit_bytes=VMEM_BYTES
        ),
        name="experts_backward",
    )(upstream, table, *weights, *kept)


def axis_peers(axis, count):
    me = lax.axis_index(axis)
    return [(offset, (me + offset) % count, {axis: (me + offset) % count}) for offset in range(1, count)]


def sender_of(axis, count, offset):
    return (lax.axis_index(axis) + count - offset) % count


def greet_all(devices):
    barrier = pltpu.get_barrier_semaphore()
    for device in devices:
        pl.semaphore_signal(barrier, inc=1, device_id=device, device_id_type=MESH)
    pl.semaphore_wait(barrier, len(devices))


def normalise(values, gain):
    scale = lax.rsqrt(jnp.mean(values * values, axis=-1, keepdims=True) + EPSILON)
    return values * scale * gain


def norm_backward(values, gain, grad):
    scale = lax.rsqrt(jnp.mean(values * values, axis=-1, keepdims=True) + EPSILON)
    spread = gain * grad
    inner = jnp.mean(values * spread, axis=-1, keepdims=True)
    gain_grad = jnp.sum(grad * values * scale, axis=0, keepdims=True)
    return scale * spread - values * (scale * scale * scale * inner), gain_grad


def allowed_pairs(sizes, seg_query, seg_key, m):
    offset = lax.axis_index("dp") * sizes.tokens
    shape = (sizes.tokens, sizes.seq)
    query_pos = lax.broadcasted_iota(jnp.int32, shape, 0) + offset
    key_pos = lax.broadcasted_iota(jnp.int32, shape, 1)
    return (key_pos <= query_pos) & (seg_query[m] == seg_key[m])


def stacked_heads(ref, sizes, m, g):
    rows = slice(m * sizes.tokens, (m + 1) * sizes.tokens)
    first = g * GROUPS
    return jnp.concatenate(
        [ref[rows, (first + h) * HEAD_DIM : (first + h + 1) * HEAD_DIM] for h in range(GROUPS)], axis=0
    )


def store_heads(ref, sizes, m, g, value):
    rows = slice(m * sizes.tokens, (m + 1) * sizes.tokens)
    for h in range(GROUPS):
        cols = slice((g * GROUPS + h) * HEAD_DIM, (g * GROUPS + h + 1) * HEAD_DIM)
        ref[rows, cols] = value[h * sizes.tokens : (h + 1) * sizes.tokens].astype(ref.dtype)


def softmax_parts(queries, keys, allowed, sizes):
    scores = dot_nt(queries, keys) * HEAD_DIM ** (-0.5)
    scores = scores.reshape(GROUPS, sizes.tokens, sizes.seq)
    scores = jnp.where(allowed[None], scores, MASKED).reshape(GROUPS * sizes.tokens, sizes.seq)
    powers = jnp.exp(scores - jnp.max(scores, axis=-1, keepdims=True))
    return powers, jnp.sum(powers, axis=-1, keepdims=True)


def attention_forward_kernel(sizes, with_table, *refs):
    refs = list(refs)
    x, seg_query, seg_key, attn_gain, ffn_gain = refs[:5]
    refs = refs[5:]
    if with_table:
        own_table = refs.pop(0)
    sources, refs = refs[:4], refs[4:]
    normed_ffn, residual, normed, queries, kv, attended = refs[:6]
    refs = refs[6:]
    if with_table:
        table = refs.pop(0)
    query_w, key_w, value_w, out_w, load_sems, kv_sent, kv_got = refs[:7]
    loads = [
        pltpu.make_async_copy(src, dst, load_sems.at[i])
        for i, (src, dst) in enumerate(zip(sources, (query_w, key_w, value_w, out_w)))
    ]
    for i in (1, 2, 0, 3):
        loads[i].start()
    place = Place(sizes)
    devices = [device for _, _, device in axis_peers("dp", sizes.copies)]
    spread = []
    if with_table:
        table_sent, table_got = refs[7:9]
        plane = axis_peers("expert", sizes.experts)
        devices += [device for _, _, device in plane]
        spread = [
            remote(
                own_table, table.at[place.z, place.x], table_sent.at[offset - 1], table_got.at[offset - 1], device
            )
            for offset, _, device in plane
        ]
    greet_all(devices)
    for copy in spread:
        copy.start()
    if with_table:
        table[place.z, place.x] = own_table[...]
    normed[...] = normalise(x[...].astype(F32), attn_gain[...]).astype(BF16)
    loads[1].wait()
    loads[2].wait()
    width = KV_HEADS * HEAD_DIM
    mine = lax.axis_index("dp")
    for part, weight in enumerate((key_w, value_w)):
        made = dot(normed[...], weight[...]).astype(BF16)
        kv[:, mine, :, part * width : (part + 1) * width] = made.reshape(sizes.micro, sizes.tokens, width)
    sends = [
        remote(kv.at[:, mine], kv.at[:, mine], kv_sent.at[offset - 1], kv_got.at[offset - 1], device)
        for offset, _, device in axis_peers("dp", sizes.copies)
    ]
    for send in sends:
        send.start()
    loads[0].wait()
    wide = 512
    for n in range(sizes.model // wide):
        cols = slice(n * wide, (n + 1) * wide)
        queries[:, cols] = dot(normed[...], query_w[:, cols]).astype(BF16)
    for offset in range(1, sizes.copies):
        theirs = sender_of("dp", sizes.copies, offset)
        block = kv.at[:, theirs]
        remote(block, block, kv_sent.at[offset - 1], kv_got.at[offset - 1], {"dp": theirs}).wait_recv()
    for m in range(sizes.micro):
        allowed = allowed_pairs(sizes, seg_query, seg_key, m)
        for g in range(KV_HEADS):
            keys = kv[m, :, :, g * HEAD_DIM : (g + 1) * HEAD_DIM].reshape(sizes.seq, HEAD_DIM)
            values = kv[m, :, :, width + g * HEAD_DIM : width + (g + 1) * HEAD_DIM].reshape(sizes.seq, HEAD_DIM)
            powers, sums = softmax_parts(stacked_heads(queries, sizes, m, g), keys, allowed, sizes)
            probs = (powers * (1.0 / sums)).astype(BF16)
            store_heads(attended, sizes, m, g, dot(probs, values))
    loads[3].wait()
    for n in range(sizes.model // wide):
        cols = slice(n * wide, (n + 1) * wide)
        residual[:, cols] = x[:, cols].astype(F32) + dot(attended[...], out_w[:, cols])
    normed_ffn[...] = normalise(residual[...], ffn_gain[...]).astype(BF16)
    for send in sends:
        send.wait_send()
    if with_table:
        for offset, _, device in plane:
            theirs = sender_of("expert", sizes.experts, offset)
            block = table.at[theirs // sizes.width, theirs % sizes.width]
            remote(
                own_table, block, table_sent.at[offset - 1], table_got.at[offset - 1], {"expert": theirs}
            ).wait_recv()
        for copy in spread:
            copy.wait_send()


def attention_forward(sizes, step, incoming, segs, gains, weights, own_table=None):
    shape = jax.ShapeDtypeStruct
    rows, model = sizes.rows, sizes.model
    kv_width = KV_HEADS * HEAD_DIM
    with_table = own_table is not None
    dma = pltpu.SemaphoreType.DMA
    outs = [
        shape((rows, model), BF16),
        shape((rows, model), F32),
        shape((rows, model), BF16),
        shape((rows, model), BF16),
        shape((sizes.micro, sizes.copies, sizes.tokens, 2 * kv_width), BF16),
        shape((rows, model), BF16),
    ]
    scratch = [
        pltpu.VMEM((model, model), BF16),
        pltpu.VMEM((model, kv_width), BF16),
        pltpu.VMEM((model, kv_width), BF16),
        pltpu.VMEM((model, model), BF16),
        dma((4,)),
        dma((sizes.copies - 1,)),
        dma((sizes.copies - 1,)),
    ]
    tables = []
    if with_table:
        tables = [own_table]
        outs.append(shape((sizes.line, sizes.width) + own_table.shape, F32))
        scratch += [dma((sizes.experts - 1,))] * 2
    return pl.pallas_call(
        functools.partial(attention_forward_kernel, sizes, with_table),
        out_shape=outs,
        in_specs=[vmem_spec()] * (5 + len(tables)) + [any_spec()] * 4,
        out_specs=[vmem_spec()] * len(outs),
        scratch_shapes=scratch,
        compiler_params=pltpu.CompilerParams(
            collective_id=4 + step, has_side_effects=True, vmem_limit_bytes=VMEM_BYTES
        ),
        name="attention_forward",
    )(incoming, *segs, *gains, *tables, *weights)


def attention_backward_kernel(
    sizes, upstream, ffn_in_grad, x, residual, queries, kv, seg_query, seg_key, attn_gain, ffn_gain,
    query_hbm, key_hbm, value_hbm, out_hbm,
    in_grad, branch_grad, query_grad, kv_grad, gain_grads,
    query_w, key_w, value_w, out_w, residual_grad, attended_grad, normed_grad, kv_part, kv_other,
    load_sems, kv_sent, kv_got,
):
    loads = [
        pltpu.make_async_copy(src, dst, load_sems.at[i])
        for i, (src, dst) in enumerate(
            ((out_hbm, out_w), (query_hbm, query_w), (key_hbm, key_w), (value_hbm, value_w))
        )
    ]
    for load in loads:
        load.start()
    peers = axis_peers("dp", sizes.copies)
    greet_all([device for _, _, device in peers])
    part, ffn_gain_grad = norm_backward(residual[...], ffn_gain[...], ffn_in_grad[...])
    total = upstream[...].astype(F32) + part
    residual_grad[...] = total
    branch_grad[...] = total.astype(BF16)
    gain_grads[1:2, :] = ffn_gain_grad
    wide = 512
    loads[0].wait()
    for n in range(sizes.model // wide):
        cols = slice(n * wide, (n + 1) * wide)
        attended_grad[:, cols] = dot_nt(branch_grad[...], out_w[cols, :]).astype(BF16)
    width = KV_HEADS * HEAD_DIM
    scale = HEAD_DIM ** (-0.5)
    mine = lax.axis_index("dp")
    for m in range(sizes.micro):
        allowed = allowed_pairs(sizes, seg_query, seg_key, m)
        for g in range(KV_HEADS):
            key_cols = slice(g * HEAD_DIM, (g + 1) * HEAD_DIM)
            value_cols = slice(width + g * HEAD_DIM, width + (g + 1) * HEAD_DIM)
            keys = kv[m, :, :, key_cols].reshape(sizes.seq, HEAD_DIM)
            values = kv[m, :, :, value_cols].reshape(sizes.seq, HEAD_DIM)
            heads = stacked_heads(queries, sizes, m, g)
            grads = stacked_heads(attended_grad, sizes, m, g)
            powers, sums = softmax_parts(heads, keys, allowed, sizes)
            probs = powers * (1.0 / sums)
            probs_grad = dot_nt(grads, values)
            score_grad = probs * (probs_grad - jnp.sum(probs_grad * probs, axis=-1, keepdims=True))
            score_grad = score_grad.astype(BF16)
            value_part = dot_tn(probs.astype(BF16), grads)
            key_part = dot_tn(score_grad, heads) * scale
            store_heads(query_grad, sizes, m, g, dot(score_grad, keys) * scale)
            shape = (sizes.copies, sizes.tokens, HEAD_DIM)
            kv_part[m, :, :, key_cols] = key_part.astype(BF16).reshape(shape)
            kv_part[m, :, :, value_cols] = value_part.astype(BF16).reshape(shape)
    sends = [
        remote(kv_part.at[:, index], kv_other.at[offset - 1], kv_sent.at[offset - 1], kv_got.at[offset - 1], device)
        for offset, index, device in peers
    ]
    for send in sends:
        send.start()
    loads[1].wait()
    loads[2].wait()
    loads[3].wait()
    summed = kv_part[:, mine].astype(F32)
    for send, (offset, _, _) in zip(sends, peers):
        send.wait_recv()
        summed += kv_other[offset - 1].astype(F32)
    kv_grad[...] = summed.reshape(sizes.rows, 2 * width).astype(BF16)
    for n in range(sizes.model // wide):
        cols = slice(n * wide, (n + 1) * wide)
        normed_grad[:, cols] = (
            dot_nt(query_grad[...], query_w[cols, :])
            + dot_nt(kv_grad[:, :width], key_w[cols, :])
            + dot_nt(kv_grad[:, width:], value_w[cols, :])
        )
    part, attn_gain_grad = norm_backward(x[...].astype(F32), attn_gain[...], normed_grad[...])
    in_grad[...] = (residual_grad[...] + part).astype(BF16)
    gain_grads[0:1, :] = attn_gain_grad
    for send in sends:
        send.wait_send()


def attention_backward(sizes, step, upstream, ffn_in_grad, x, kept, segs, gains, weights):
    shape = jax.ShapeDtypeStruct
    rows, model = sizes.rows, sizes.model
    kv_width = KV_HEADS * HEAD_DIM
    residual, _, queries, kv, _ = kept
    dma = pltpu.SemaphoreType.DMA
    return pl.pallas_call(
        functools.partial(attention_backward_kernel, sizes),
        out_shape=[
            shape((rows, model), BF16),
            shape((rows, model), BF16),
            shape((rows, model), BF16),
            shape((rows, 2 * kv_width), BF16),
            shape((2, model), F32),
        ],
        in_specs=[vmem_spec()] * 10 + [any_spec()] * 4,
        out_specs=[vmem_spec()] * 5,
        scratch_shapes=[
            pltpu.VMEM((model, model), BF16),
            pltpu.VMEM((model, kv_width), BF16),
            pltpu.VMEM((model, kv_width), BF16),
            pltpu.VMEM((model, model), BF16),
            pltpu.VMEM((rows, model), F32),
            pltpu.VMEM((rows, model), BF16),
            pltpu.VMEM((rows, model), F32),
            pltpu.VMEM((sizes.micro, sizes.copies, sizes.tokens, 2 * kv_width), BF16),
            pltpu.VMEM((sizes.copies - 1, sizes.micro, sizes.tokens, 2 * kv_width), BF16),
            dma((4,)),
            dma((sizes.copies - 1,)),
            dma((sizes.copies - 1,)),
        ],
        compiler_params=pltpu.CompilerParams(
            collective_id=6 + step, has_side_effects=True, vmem_limit_bytes=VMEM_BYTES
        ),
        name="attention_backward",
    )(upstream, ffn_in_grad, x, residual, queries, kv, *segs, *gains, *weights)


class Axis:
    def __init__(self, count, me, device):
        self.count, self.me, self.device = count, me, device

    def peers(self):
        return [(offset - 1, (self.me + offset) % self.count) for offset in range(1, self.count)]

    def senders(self):
        return [(offset - 1, (self.me + self.count - offset) % self.count) for offset in range(1, self.count)]


def add_rows(dst, sources, rows):
    def step(i, carry):
        at = pl.ds(pl.multiple_of(i * 16, 16), 16)
        acc = dst[at, :].astype(F32)
        for source in sources:
            acc += source[at, :].astype(F32)
        dst[at, :] = acc.astype(BF16)
        return carry

    lax.fori_loop(0, rows // 16, step, 0)


class Unit:
    def __init__(self, half, axes, line, place_index, grad, total, crossed, sems):
        self.half, self.grad, self.total = half, grad, total
        self.first, self.second = axes if half == 0 else axes[::-1]
        self.line, self.at = line, place_index
        self.crossed, self.sems = crossed, sems
        self.rows = grad.shape[3]
        self.part = grad.shape[4] // line.count

    def side(self, ref, first):
        return ref.at[first, :, 0] if self.half == 0 else ref.at[:, first, 1]

    def block(self, ref, second):
        y, x = self.at
        return ref.at[y, second, 0] if self.half == 0 else ref.at[second, x, 1]

    def piece(self, ref, z):
        y, x = self.at
        return ref.at[y, x, self.half, :, pl.ds(pl.multiple_of(z * self.part, 128), self.part)]

    def plan(self, stage):
        axis = (self.first, self.second, self.line, self.line, self.second, self.first)[stage]
        view = (self.side, self.block, self.piece, self.piece, self.block, self.side)[stage]
        return axis, view, self.sems[2 * stage], self.sems[2 * stage + 1]

    def sends(self, stage):
        axis, view, sent, got = self.plan(stage)
        for slot, peer in axis.peers():
            if stage < 3:
                source, land = view(self.grad, peer), self.crossed[stage].at[slot]
            else:
                source = land = view(self.total, axis.me)
            yield remote(source, land, sent.at[slot], got.at[slot], axis.device(peer))

    def arrivals(self, stage):
        axis, view, sent, got = self.plan(stage)
        for slot, sender in axis.senders():
            land = self.crossed[stage].at[slot] if stage < 3 else view(self.total, sender)
            yield remote(land, land, sent.at[slot], got.at[slot], axis.device(sender))

    def start(self, stage):
        for copy in self.sends(stage):
            copy.start()

    def arrive(self, stage):
        for copy in self.arrivals(stage):
            copy.wait_recv()

    def finish(self, stage):
        for copy in self.sends(stage):
            copy.wait_send()

    def add(self, stage):
        crossed = self.crossed[stage]
        slots = range(crossed.shape[0])
        if stage == 0:
            held = self.side(self.grad, self.first.me)
            for other in range(self.second.count):
                add_rows(held.at[other], [crossed.at[slot, other] for slot in slots], self.rows)
        elif stage == 1:
            add_rows(self.block(self.grad, self.second.me), [crossed.at[slot] for slot in slots], self.rows)
        else:
            source, target = self.piece(self.grad, self.line.me), self.piece(self.total, self.line.me)

            def step(i, carry):
                at = pl.ds(pl.multiple_of(i * 16, 16), 16)
                acc = source[at, :].astype(F32)
                for slot in slots:
                    acc += crossed[slot, at, :].astype(F32)
                target[at, :] = acc.astype(BF16)
                return carry

            lax.fori_loop(0, self.rows // 16, step, 0)


STAGES = 6


def reduce_kernel(sizes, active, prior, *refs):
    refs = list(refs)
    normed, attended, branch_grad, query_grad, kv_grad, gains = refs[:6]
    expert_hbm = refs[6:9]
    refs = refs[9 + prior:]
    dense_out, gains_out, expert_out = refs[:3], refs[3], refs[4:7]
    refs = refs[7:]
    grads, totals, refs = refs[:3], refs[3:6], refs[6:]
    crossed, refs = refs[:18], refs[18:]
    expert_got, expert_own, refs = refs[:3], refs[3:6], refs[6:]
    gain_slots, gain_sum, refs = refs[:3], refs[3], refs[4:]
    out_sems, own_sems, expert_sent, expert_come, gain_sent, gain_got = refs[:6]
    unit_sems = refs[6:]

    @pl.when(lax.axis_index("section") == active)
    def _():
        place = Place(sizes)
        along_y = Axis(sizes.copies, lax.axis_index("dp"), lambda i: {"dp": i})
        along_x = Axis(sizes.width, place.x, lambda i: place.device(place.z, i))
        along_z = Axis(sizes.line, place.z, lambda i: place.device(i, place.x))
        axes = (along_y, along_x, along_z)
        greet_all([axis.device(peer) for axis in axes for _, peer in axis.peers()])
        shape = (sizes.copies, sizes.width, 2, sizes.model // (2 * sizes.copies * sizes.width))
        units = []
        for t in range(3):
            cols = grads[t].shape[1]
            grad, total = grads[t].reshape(*shape, cols), totals[t].reshape(*shape, cols)
            units.append(
                [
                    Unit(
                        half, (along_y, along_x), along_z, (along_y.me, place.x), grad, total,
                        crossed[6 * t + 3 * half : 6 * t + 3 * half + 3],
                        unit_sems[(2 * t + half) * 2 * STAGES : (2 * t + half + 1) * 2 * STAGES],
                    )
                    for half in range(2)
                ]
            )
        own_loads = []
        cuts = (0, 0, 1)
        share = sizes.model // sizes.copies

        def slab(ref, cut, y):
            at = pl.ds(pl.multiple_of(y * share, 128), share)
            return ref.at[at, :] if cut == 0 else ref.at[:, at]

        for i in range(3):
            own_loads.append(
                pltpu.make_async_copy(slab(expert_hbm[i], cuts[i], along_y.me), expert_own[i], own_sems.at[i])
            )
            own_loads[-1].start()
        expert_copies = [
            remote(
                slab(expert_hbm[i], cuts[i], peer), expert_got[i].at[slot], expert_sent.at[i, slot],
                expert_come.at[i, slot], along_y.device(peer),
            )
            for i in range(3)
            for slot, peer in along_y.peers()
        ]

        def gain_copy(stage, slot, row, device):
            return remote(
                gain_sum.at[stage], gain_slots[stage].at[row], gain_sent.at[stage, slot], gain_got.at[stage, slot],
                device,
            )

        def gain_sends(stage):
            axis = axes[stage]
            return [gain_copy(stage, slot, axis.me, axis.device(peer)) for slot, peer in axis.peers()]

        def gain_start(stage):
            gain_slots[stage][axes[stage].me] = gain_sum[stage]
            for copy in gain_sends(stage):
                copy.start()

        def gain_end(stage):
            for slot, sender in axes[stage].senders():
                gain_copy(stage, slot, sender, axes[stage].device(sender)).wait_recv()
            acc = gain_slots[stage][0]
            for i in range(1, axes[stage].count):
                acc += gain_slots[stage][i]
            gain_sum[stage + 1] = acc

        gain_sum[0] = gains[...]
        gain_start(0)
        lefts, rights = (attended, normed, normed), (branch_grad, query_grad, kv_grad)

        def make(t):
            cols = grads[t].shape[1]
            wide = 512

            def step(i, carry):
                at = pl.ds(pl.multiple_of(i * 256, 256), 256)
                for n in range(cols // wide):
                    span = slice(n * wide, (n + 1) * wide)
                    grads[t][at, span] = dot_tn(lefts[t][:, at], rights[t][:, span]).astype(BF16)
                return carry

            lax.fori_loop(0, sizes.model // 256, step, 0)

        out_copies = [pltpu.make_async_copy(totals[t], dense_out[t], out_sems.at[t]) for t in range(3)]
        for tick in range(STAGES + 1 + 2):
            for t in range(3):
                stage = tick - t
                if stage < 0 or stage > STAGES:
                    continue
                if stage == 0:
                    make(t)
                for unit in units[t]:
                    if stage > 0:
                        unit.arrive(stage - 1)
                        if stage <= 3:
                            unit.add(stage - 1)
                    if stage < STAGES:
                        unit.start(stage)
                if stage == STAGES:
                    out_copies[t].start()
            if 1 <= tick <= 3:
                gain_end(tick - 1)
                if tick < 3:
                    gain_start(tick)
            if tick == 2:
                for copy in expert_copies:
                    copy.start()
            if tick == 5:
                for load in own_loads:
                    load.wait()
                for copy in expert_copies:
                    copy.wait_recv()
                for i in range(3):
                    add_rows(
                        expert_own[i], [expert_got[i].at[slot] for slot in range(sizes.copies - 1)],
                        expert_own[i].shape[0],
                    )
                    pltpu.make_async_copy(expert_own[i], expert_out[i], own_sems.at[i]).start()
        gains_copy = pltpu.make_async_copy(gain_sum.at[3], gains_out, out_sems.at[3])
        gains_copy.start()
        for stage in range(STAGES):
            for t in range(3):
                for unit in units[t]:
                    unit.finish(stage)
        for stage in range(3):
            for copy in gain_sends(stage):
                copy.wait_send()
        for copy in expert_copies:
            copy.wait_send()
        for copy in out_copies:
            copy.wait()
        for i in range(3):
            pltpu.make_async_copy(expert_own[i], expert_out[i], own_sems.at[i]).wait()
        gains_copy.wait()


def reduce_grads(sizes, active, operands, experts, prior):
    shape = jax.ShapeDtypeStruct
    model, hidden = sizes.model, sizes.hidden
    copies, width, line = sizes.copies, sizes.width, sizes.line
    kv_width = 2 * KV_HEADS * HEAD_DIM
    share = model // copies
    half_rows = model // (2 * copies * width)
    dma = pltpu.SemaphoreType.DMA
    columns = (model, model, kv_width)
    outs = [shape((model, cols), BF16) for cols in columns]
    outs.append(shape((8, model), F32))
    outs += [shape((share, hidden), BF16), shape((share, hidden), BF16), shape((hidden, share), BF16)]
    crossed, unit_sems = [], []
    for cols in columns:
        for half in range(2):
            first, second = (copies, width) if half == 0 else (width, copies)
            crossed += [
                pltpu.VMEM((first - 1, second, half_rows, cols), BF16),
                pltpu.VMEM((second - 1, half_rows, cols), BF16),
                pltpu.VMEM((line - 1, half_rows, cols // line), BF16),
            ]
            counts = (first, second, line, line, second, first)
            unit_sems += [dma((count - 1,)) for count in counts for _ in range(2)]
    scratch = [pltpu.VMEM((model, cols), BF16) for cols in columns] * 2
    scratch += crossed
    slabs = [(share, hidden), (share, hidden), (hidden, share)]
    scratch += [pltpu.VMEM((copies - 1,) + slab, BF16) for slab in slabs]
    scratch += [pltpu.VMEM(slab, BF16) for slab in slabs]
    scratch += [pltpu.VMEM((count, 8, model), F32) for count in (copies, width, line)]
    scratch += [pltpu.VMEM((4, 8, model), F32)]
    most = max(copies, width, line) - 1
    scratch += [dma((4,)), dma((3,)), dma((3, copies - 1)), dma((3, copies - 1)), dma((3, most)), dma((3, most))]
    scratch += unit_sems
    aliases = {9 + i: i for i in range(len(prior))}
    return pl.pallas_call(
        functools.partial(reduce_kernel, sizes, active, len(prior)),
        out_shape=outs,
        in_specs=[vmem_spec()] * 6 + [any_spec()] * (3 + len(prior)),
        out_specs=[any_spec()] * 7,
        scratch_shapes=scratch,
        input_output_aliases=aliases,
        compiler_params=pltpu.CompilerParams(
            collective_id=8 + active, has_side_effects=True, vmem_limit_bytes=VMEM_BYTES
        ),
        name="reduce_grads",
    )(*operands, *experts, *prior)


def routing_table(sizes, expert_ids, route_weights):
    named = expert_ids[None] == jnp.arange(sizes.experts, dtype=jnp.int32)[:, None, None, None]
    used = jnp.any(named, axis=-1)
    weight = jnp.sum(jnp.where(named, route_weights[None], 0.0), axis=-1)
    before = jnp.triu(jnp.ones((sizes.tokens, sizes.tokens), BF16), 1)
    rank = jnp.where(used, dot(used.astype(BF16), before), -1.0)
    return jnp.concatenate([rank, weight], axis=1)


def per_device(
    boundary, w_query, w_key, w_value, w_out, norm_attn, norm_ffn, w_gate, w_up, w_down,
    expert_ids, route_weights, segments,
):
    micro, tokens, model = boundary.shape[1:]
    sizes = Sizes(lax.axis_size("expert"), lax.axis_size("dp"), micro, tokens, model, w_gate.shape[-1])
    first = lax.axis_index("section") == 0
    weights = (w_query[0], w_key[0], w_value[0], w_out[0])
    gains = (norm_attn, norm_ffn)
    expert_params = (w_gate[0, 0], w_up[0, 0], w_down[0, 0])
    own_table = routing_table(sizes, expert_ids[0], route_weights[0])
    offset = lax.axis_index("dp") * tokens
    query_seg = lax.dynamic_slice_in_dim(segments, offset, tokens, axis=1)
    segs = (query_seg[:, :, None], segments[:, None, :])
    own_rows = boundary[0].reshape(sizes.rows, model)

    def forward(step, incoming, table):
        normed_ffn, *stored = attention_forward(
            sizes, step, incoming, segs, gains, weights, own_table if step == 0 else None
        )
        if step == 0:
            table = stored.pop()
        mixed, *kept = experts_forward(sizes, step, normed_ffn, table, expert_params)
        return (stored[0] + mixed).astype(BF16), stored, kept, table

    def backward(step, upstream, incoming, stored, kept, table):
        ffn_in_grad, *expert_grads = experts_backward(sizes, step, upstream, table, expert_params, kept)
        in_grad, branch_grad, query_grad, kv_grad, gain_grads = attention_backward(
            sizes, step, upstream, ffn_in_grad, incoming, stored, segs, gains, weights
        )
        gain_grads = jnp.pad(gain_grads, ((0, 6), (0, 0)))
        return in_grad, (stored[1], stored[4], branch_grad, query_grad, kv_grad, gain_grads), expert_grads

    out_0, stored_0, kept_0, table = forward(0, own_rows, None)
    received = lax.ppermute(out_0, "section", [(0, 1)])
    out_1, stored_1, kept_1, _ = forward(1, received, table)
    in_grad_1, dense_1, expert_1 = backward(1, own_rows, received, stored_1, kept_1, table)
    upstream_0 = lax.ppermute(in_grad_1, "section", [(1, 0)])
    sums = reduce_grads(sizes, 1, dense_1, expert_1, ())
    in_grad_0, dense_0, expert_0 = backward(0, upstream_0, own_rows, stored_0, kept_0, table)
    sums = reduce_grads(sizes, 0, dense_0, expert_0, tuple(sums))

    def choose(a, b):
        return jnp.where(first, a, b).reshape(1, micro, tokens, model)

    kv_width = KV_HEADS * HEAD_DIM
    out_sum, query_sum, kv_sum, gain_sum, gate_sum, up_sum, down_sum = sums
    return (
        choose(out_0, out_1),
        choose(in_grad_0, in_grad_1),
        query_sum.astype(F32)[None],
        kv_sum[:, :kv_width].astype(F32)[None],
        kv_sum[:, kv_width:].astype(F32)[None],
        out_sum.astype(F32)[None],
        gain_sum[0][None],
        gain_sum[1][None],
        gate_sum.astype(F32)[None, None],
        up_sum.astype(F32)[None, None],
        down_sum.astype(F32)[None, None],
    )


def solution(mesh):
    in_specs = (
        P("section", None, ("expert", "dp"), None),
        P("section", None, None),
        P("section", None, None),
        P("section", None, None),
        P("section", None, None),
        P("section", None),
        P("section", None),
        P("section", "expert", None, None),
        P("section", "expert", None, None),
        P("section", "expert", None, None),
        P("section", None, ("expert", "dp"), None),
        P("section", None, ("expert", "dp"), None),
        P(None, "expert"),
    )
    out_specs = (
        P("section", None, ("expert", "dp"), None),
        P("section", None, ("expert", "dp"), None),
        P("section", None, None),
        P("section", None, None),
        P("section", None, None),
        P("section", None, None),
        P("section", None),
        P("section", None),
        P("section", "expert", "dp", None),
        P("section", "expert", "dp", None),
        P("section", "expert", None, "dp"),
    )
    return jax.shard_map(
        per_device, mesh=mesh, in_specs=in_specs, out_specs=out_specs, check_vma=False
    )
```

```python
import functools

import jax
import jax.numpy as jnp
from jax import lax
from jax.experimental import pallas as pl
from jax.experimental.pallas import tpu as pltpu
from jax.sharding import PartitionSpec as P

HEADS = 12
KV_HEADS = 2
HEAD_DIM = 128
GROUPS = HEADS // KV_HEADS
TOP = 4
LINE = 4
EPSILON = 1e-06
MASKED = -1e30
F32 = jnp.float32
BF16 = jnp.bfloat16
MESH = pl.DeviceIdType.MESH
VMEM_BYTES = 60 * 1024 * 1024
TILE = 256
WIDE = 512
GELU_A = 0.7978845608028654
GELU_B = 0.044715


def dot(a, b):
    return jnp.dot(a, b, preferred_element_type=F32)


def dot_nt(a, b):
    return lax.dot_general(a, b, (((1,), (1,)), ((), ())), preferred_element_type=F32)


def dot_tn(a, b):
    return lax.dot_general(a, b, (((0,), (0,)), ((), ())), preferred_element_type=F32)


def rms_norm(values, scales):
    return values * lax.rsqrt(jnp.mean(values * values, axis=-1, keepdims=True) + EPSILON) * scales


class Sizes:
    def __init__(self, experts, copies, micro, tokens, model, hidden):
        self.experts, self.copies, self.micro, self.tokens = experts, copies, micro, tokens
        self.model, self.hidden = model, hidden
        self.seq = copies * tokens
        self.line = LINE
        self.width = experts // LINE
        self.cap = 3 * tokens * TOP // (2 * experts)
        self.packed = micro * self.cap
        self.group = self.width * self.packed
        self.rows = micro * tokens
        self.out_units = model // WIDE
        self.units = 2 * self.out_units + 1
        self.share = model // copies


class Place:
    def __init__(self, sizes):
        self.sizes = sizes
        self.me = lax.axis_index("expert")
        self.z = self.me // sizes.width
        self.x = self.me % sizes.width

    def device(self, z, x):
        return {"expert": z * self.sizes.width + x}

    def above(self):
        return self.device(self.z + 1, self.x)

    def below(self):
        return self.device(self.z - 1, self.x)

    def peer_x(self, offset):
        return (self.x + offset) % self.sizes.width

    def near(self, step):
        z = self.z
        middle_low = jnp.where(step < 2, 1 - step, step)
        middle_high = jnp.where(step < 2, 2 + step, 3 - step)
        return jnp.where(
            z == 0, step, jnp.where(z == 3, 3 - step, jnp.where(z == 1, middle_low, middle_high))
        )

    def far(self, step):
        return self.near(self.sizes.line - 1 - step)


def remote(src, dst, send, recv, device):
    return pltpu.make_async_remote_copy(
        src_ref=src, dst_ref=dst, send_sem=send, recv_sem=recv, device_id=device, device_id_type=MESH
    )


def greet(place, others=()):
    line, width = place.sizes.line, place.sizes.width
    barrier = pltpu.get_barrier_semaphore()

    @pl.when(place.z > 0)
    def _():
        pl.semaphore_signal(barrier, inc=1, device_id=place.below(), device_id_type=MESH)

    @pl.when(place.z < line - 1)
    def _():
        pl.semaphore_signal(barrier, inc=1, device_id=place.above(), device_id_type=MESH)

    for offset in range(1, width):
        pl.semaphore_signal(
            barrier, inc=1, device_id=place.device(place.z, place.peer_x(offset)), device_id_type=MESH
        )
    for device in others:
        pl.semaphore_signal(barrier, inc=1, device_id=device, device_id_type=MESH)
    count = (width - 1) + len(others) + (place.z > 0).astype(jnp.int32) + (place.z < line - 1).astype(jnp.int32)
    pl.semaphore_wait(barrier, count)


class Routing:
    def __init__(self, place, table):
        self.place, self.table = place, table

    def hits(self, zz, xx, expert_x, m):
        sizes = self.place.sizes
        rows = self.table[zz, xx, self.place.z * sizes.width + expert_x, m]
        wanted = lax.broadcasted_iota(jnp.int32, (sizes.cap, sizes.tokens), 0).astype(F32)
        return rows[0:1] == wanted, rows[1:2]

    def selector(self, zz, expert_x, m):
        hit, _ = self.hits(zz, self.place.x, expert_x, m)
        return jnp.where(hit, 1.0, 0.0).astype(BF16)

    def weights(self, zz):
        sizes = self.place.sizes
        parts = []
        for xx in range(sizes.width):
            for m in range(sizes.micro):
                hit, weight = self.hits(zz, xx, self.place.x, m)
                parts.append(jnp.sum(jnp.where(hit, weight, 0.0), axis=1, keepdims=True))
        return jnp.concatenate(parts, axis=0)


class Gather:
    def __init__(self, place, routing, line, stage, packed, sems):
        self.place, self.routing, self.line, self.stage, self.packed = place, routing, line, stage, packed
        self.line_up, self.line_down, self.line_got, self.x_sent, self.x_got = sems

    def up(self, zz, m):
        block = self.line.at[zz, m]
        return remote(block, block, self.line_up.at[zz, m], self.line_got.at[zz, m], self.place.above())

    def down(self, zz, m):
        block = self.line.at[zz, m]
        return remote(block, block, self.line_down.at[zz, m], self.line_got.at[zz, m], self.place.below())

    def across(self, zz, offset, m):
        place = self.place
        return remote(
            self.stage.at[zz, offset - 1, m],
            self.packed.at[zz, place.x, m],
            self.x_sent.at[zz, offset - 1, m],
            self.x_got.at[zz, offset - 1, m],
            place.device(place.z, place.peer_x(offset)),
        )

    def pack(self, zz, expert_x, m):
        return dot(self.routing.selector(zz, expert_x, m), self.line[zz, m]).astype(BF16)

    def relays_up(self, zz):
        return (zz <= self.place.z) & (self.place.z < self.place.sizes.line - 1)

    def relays_down(self, zz):
        return (zz >= self.place.z) & (self.place.z > 0)

    def fetch(self, zz):
        place, sizes = self.place, self.place.sizes
        for m in range(sizes.micro):

            @pl.when(zz != place.z)
            def _():
                self.up(zz, m).wait_recv()

            @pl.when(self.relays_up(zz))
            def _():
                self.up(zz, m).start()

            @pl.when(self.relays_down(zz))
            def _():
                self.down(zz, m).start()

            for offset in range(1, sizes.width):
                self.stage[zz, offset - 1, m] = self.pack(zz, place.peer_x(offset), m)
                self.across(zz, offset, m).start()
        for m in range(sizes.micro):
            self.packed[zz, place.x, m] = self.pack(zz, place.x, m)

    def run(self, own, compute):
        place, sizes = self.place, self.place.sizes
        line = sizes.line
        self.line[place.z] = own[...]
        ends = (place.z == 0) | (place.z == line - 1)

        def step(i, carry):
            at_ends = ((i < 2) | (i == 3) | (i == 5)).astype(jnp.int32)
            at_middle = ((i < 3) | (i == 4)).astype(jnp.int32)
            fetches = jnp.where(ends, at_ends, at_middle)
            before_ends = jnp.where(i < 2, i, jnp.minimum(i // 2 + 1, line))
            before_middle = jnp.where(i < 4, i, jnp.minimum(i - 1, line))
            before = jnp.where(ends, before_ends, before_middle)

            @pl.when(fetches == 1)
            def _():
                self.fetch(place.near(before))

            @pl.when(fetches == 0)
            def _():
                zz = place.near(i - before)
                for m in range(sizes.micro):
                    for offset in range(1, sizes.width):
                        self.across(zz, offset, m).wait_recv()
                compute(zz)

            return carry

        lax.fori_loop(0, 2 * line, step, 0)

        def finish(zz, carry):
            for m in range(sizes.micro):

                @pl.when(self.relays_up(zz))
                def _():
                    self.up(zz, m).wait_send()

                @pl.when(self.relays_down(zz))
                def _():
                    self.down(zz, m).wait_send()

                for offset in range(1, sizes.width):
                    self.across(zz, offset, m).wait_send()
            return carry

        lax.fori_loop(0, line, finish, 0)


class Scatter:
    def __init__(self, place, routing, results, crossed, up_in, down_in, chain, total, out, sems):
        self.place, self.routing, self.results, self.crossed = place, routing, results, crossed
        self.up_in, self.down_in, self.chain, self.total, self.out = up_in, down_in, chain, total, out
        self.x_sent, self.x_got, self.up_sent, self.up_got, self.down_sent, self.down_got = sems

    def across(self, zz, offset, m):
        place = self.place
        return remote(
            self.results.at[zz, place.peer_x(offset), m],
            self.crossed.at[zz, offset - 1, m],
            self.x_sent.at[zz, offset - 1, m],
            self.x_got.at[zz, offset - 1, m],
            place.device(place.z, place.peer_x(offset)),
        )

    def up(self, zz, m):
        return remote(
            self.chain.at[zz, m], self.up_in.at[zz, m], self.up_sent.at[zz, m], self.up_got.at[zz, m],
            self.place.above(),
        )

    def down(self, zz, m):
        return remote(
            self.chain.at[zz, m], self.down_in.at[zz, m], self.down_sent.at[zz, m], self.down_got.at[zz, m],
            self.place.below(),
        )

    def run(self, side):
        place, sizes = self.place, self.place.sizes
        line, width, micro = sizes.line, sizes.width, sizes.micro

        def launch(k, carry):
            zz = place.far(k)
            for m in range(micro):
                for offset in range(1, width):
                    self.across(zz, offset, m).start()
            return carry

        lax.fori_loop(0, line, launch, 0)

        def step(j, carry):
            side(j)
            zz, m = place.far(j // micro), j % micro
            acc = dot_tn(self.routing.selector(zz, place.x, m), self.results[zz, place.x, m])
            for offset in range(1, width):
                sender = (place.x + width - offset) % width
                pick = self.routing.selector(zz, sender, m)
                self.across(zz, offset, m).wait_recv()
                acc += dot_tn(pick, self.crossed[zz, offset - 1, m])
            self.total[...] = acc

            @pl.when((zz >= place.z) & (place.z > 0))
            def _():
                self.up(zz, m).wait_recv()
                self.total[...] += self.up_in[zz, m].astype(F32)

            @pl.when((zz <= place.z) & (place.z < line - 1))
            def _():
                self.down(zz, m).wait_recv()
                self.total[...] += self.down_in[zz, m].astype(F32)

            @pl.when(zz == place.z)
            def _():
                self.out[m] = self.total[...]

            @pl.when(zz != place.z)
            def _():
                self.chain[zz, m] = self.total[...].astype(BF16)

            @pl.when(zz > place.z)
            def _():
                self.up(zz, m).start()

            @pl.when(zz < place.z)
            def _():
                self.down(zz, m).start()

            return carry

        lax.fori_loop(0, line * micro, step, 0)

        def finish(zz, carry):
            for m in range(micro):
                for offset in range(1, width):
                    self.across(zz, offset, m).wait_send()

                @pl.when(zz > place.z)
                def _():
                    self.up(zz, m).wait_send()

                @pl.when(zz < place.z)
                def _():
                    self.down(zz, m).wait_send()

            return carry

        lax.fori_loop(0, line, finish, 0)


def gelu_parts(gate):
    inner = GELU_A * (gate + GELU_B * gate * gate * gate)
    tanh = jnp.tanh(inner)
    value = 0.5 * gate * (1.0 + tanh)
    slope = 0.5 * (1.0 + tanh) + 0.5 * gate * (1.0 - tanh * tanh) * (
        GELU_A * (1.0 + 3.0 * GELU_B * gate * gate)
    )
    return value, slope


def is_section(active):
    return lax.axis_index("section") == active


def vmem_spec():
    return pl.BlockSpec(memory_space=pltpu.VMEM)


def any_spec():
    return pl.BlockSpec(memory_space=pl.ANY)


def shape(dims, dtype):
    return jax.ShapeDtypeStruct(dims, dtype)


class Buffers:
    def __init__(self, sizes):
        line, width, micro = sizes.line, sizes.width, sizes.micro
        dma = pltpu.SemaphoreType.DMA
        self.block = (micro, sizes.tokens, sizes.model)
        self.lines = (line,) + self.block
        self.packed = (line, width, micro, sizes.cap, sizes.model)
        self.crossed = (line, width - 1, micro, sizes.cap, sizes.model)
        self.hidden = (line, sizes.group, sizes.hidden)
        self.wide_weight = (sizes.model, sizes.hidden)
        self.tall_weight = (sizes.hidden, sizes.model)
        across = dma((line, width - 1, micro))
        along = dma((line, micro))
        self.gather_sems = [along, along, along, across, across]
        self.scatter_sems = [across, across, along, along, along, along]
        self.gather = [pltpu.VMEM(self.lines, BF16), pltpu.VMEM(self.crossed, BF16)]
        self.scatter = [
            pltpu.VMEM(self.packed, BF16),
            pltpu.VMEM(self.crossed, BF16),
            pltpu.VMEM(self.lines, BF16),
            pltpu.VMEM(self.lines, BF16),
            pltpu.VMEM(self.block[1:], F32),
        ]


def expert_call(kernel, collective, ins, outs, scratch, operands, name):
    return pl.pallas_call(
        kernel,
        out_shape=[one for one, _ in outs],
        in_specs=[vmem_spec() if held else any_spec() for held in ins],
        out_specs=[vmem_spec() if held else any_spec() for _, held in outs],
        scratch_shapes=scratch,
        compiler_params=pltpu.CompilerParams(
            collective_id=collective, has_side_effects=True, vmem_limit_bytes=VMEM_BYTES
        ),
        name=name,
    )(*operands)


def copies_of(pairs, sems):
    return [pltpu.make_async_copy(src, dst, sems.at[i]) for i, (src, dst) in enumerate(pairs)]


def begin_kernel(
    sizes, active, own, own_table, table, packed_hbm, own_held, line, stage, packed, load_sems,
    table_sent, table_got, *sems,
):
    place = Place(sizes)
    peers = axis_peers("expert", sizes.experts)
    load = pltpu.make_async_copy(own, own_held, load_sems.at[0])

    @pl.when(is_section(active))
    def _():
        load.start()

    greet_all([device for _, _, device in peers])
    sends = [
        remote(own_table, table.at[place.z, place.x], table_sent.at[offset - 1], table_got.at[offset - 1], device)
        for offset, _, device in peers
    ]
    for send in sends:
        send.start()
    table[place.z, place.x] = own_table[...]
    for offset, _, _ in peers:
        theirs = sender_of("expert", sizes.experts, offset)
        block = table.at[theirs // sizes.width, theirs % sizes.width]
        remote(
            own_table, block, table_sent.at[offset - 1], table_got.at[offset - 1], {"expert": theirs}
        ).wait_recv()

    @pl.when(is_section(active))
    def _():
        load.wait()
        Gather(place, Routing(place, table), line, stage, packed, sems).run(own_held, lambda zz: None)
        keep = pltpu.make_async_copy(packed, packed_hbm, load_sems.at[0])
        keep.start()
        keep.wait()

    for send in sends:
        send.wait_send()


def begin(sizes, active, own, own_table):
    hold = Buffers(sizes)
    dma = pltpu.SemaphoreType.DMA
    return expert_call(
        functools.partial(begin_kernel, sizes, active),
        0,
        (False, True),
        [
            (shape((sizes.line, sizes.width) + own_table.shape, F32), True),
            (shape(hold.packed, BF16), False),
        ],
        [pltpu.VMEM(hold.block, BF16)]
        + hold.gather
        + [pltpu.VMEM(hold.packed, BF16), dma((1,))]
        + [dma((sizes.experts - 1,))] * 2
        + hold.gather_sems,
        (own, own_table),
        "begin",
    )


def send_back(place, routing, buffers, line, out, sems, side):
    results, crossed, up_in, down_in, total = buffers
    Scatter(place, routing, results, crossed, up_in, down_in, line, total, out, sems).run(side)


def experts_forward_kernel(
    sizes, active, own, table, gate_hbm, up_hbm, down_hbm,
    out, packed_hbm, gates_hbm, ups_hbm,
    gate_w, up_w, down_w, packed, gates, ups, acts, load_sems, keep_sems, line, stage, *rest,
):
    buffers, gather_sems, scatter_sems = rest[:5], rest[5:10], rest[10:]
    results = buffers[0]

    @pl.when(is_section(active))
    def _():
        place = Place(sizes)
        loads = copies_of(((gate_hbm, gate_w), (up_hbm, up_w), (down_hbm, down_w)), load_sems)
        for load in loads:
            load.start()
        greet(place)
        routing = Routing(place, table)
        gather = Gather(place, routing, line, stage, packed, gather_sems)

        def compute(zz):
            @pl.when(zz == place.z)
            def _():
                for load in loads:
                    load.wait()

            rows = packed[zz].reshape(sizes.group, sizes.model)
            for f in range(sizes.hidden // TILE):
                cols = slice(f * TILE, (f + 1) * TILE)
                gate = dot(rows, gate_w[:, cols])
                up = dot(rows, up_w[:, cols])
                gates[zz, :, cols] = gate.astype(BF16)
                ups[zz, :, cols] = up.astype(BF16)
                value, _ = gelu_parts(gate)
                acts[:, cols] = (value * up).astype(BF16)
            weight = routing.weights(zz)
            for n in range(sizes.model // WIDE):
                cols = slice(n * WIDE, (n + 1) * WIDE)
                made = dot(acts[...], down_w[:, cols]) * weight
                results[zz, :, :, :, cols] = made.astype(BF16).reshape(
                    sizes.width, sizes.micro, sizes.cap, WIDE
                )

        gather.run(own, compute)
        keeps = copies_of(((packed, packed_hbm), (gates, gates_hbm), (ups, ups_hbm)), keep_sems)
        for keep in keeps:
            keep.start()
        send_back(place, routing, buffers, line, out, scatter_sems, lambda j: None)
        for keep in keeps:
            keep.wait()


def experts_forward(sizes, active, normed, table, weights):
    hold = Buffers(sizes)
    dma = pltpu.SemaphoreType.DMA
    return expert_call(
        functools.partial(experts_forward_kernel, sizes, active),
        1,
        (True, True, False, False, False),
        [
            (shape(hold.block, F32), True),
            (shape(hold.packed, BF16), False),
            (shape(hold.hidden, BF16), False),
            (shape(hold.hidden, BF16), False),
        ],
        [
            pltpu.VMEM(hold.wide_weight, BF16),
            pltpu.VMEM(hold.wide_weight, BF16),
            pltpu.VMEM(hold.tall_weight, BF16),
            pltpu.VMEM(hold.packed, BF16),
            pltpu.VMEM(hold.hidden, BF16),
            pltpu.VMEM(hold.hidden, BF16),
            pltpu.VMEM(hold.hidden[1:], BF16),
            dma((3,)),
            dma((3,)),
        ]
        + hold.gather
        + hold.scatter
        + hold.gather_sems
        + hold.scatter_sems,
        (normed, table, *weights),
        "experts_forward",
    )


def store_row_grads(sizes, results, zz, gates, ups, gate_w, up_w):
    for n in range(sizes.model // WIDE):
        cols = slice(n * WIDE, (n + 1) * WIDE)
        made = dot_nt(gates[zz], gate_w[cols, :]) + dot_nt(ups[zz], up_w[cols, :])
        results[zz, :, :, :, cols] = made.astype(BF16).reshape(sizes.width, sizes.micro, sizes.cap, WIDE)


def weight_grads_step(sizes, packed, grads, gates, ups, acts, gate_grad, up_grad, down_grad):
    total_rows = sizes.line * sizes.group

    def part(j):
        @pl.when(j < sizes.model // TILE)
        def _():
            cols = pl.ds(pl.multiple_of(j * TILE, TILE), TILE)
            rows = packed[:, :, :, :, cols].reshape(total_rows, TILE)
            gate_grad[cols, :] = dot_tn(rows, gates[...].reshape(total_rows, sizes.hidden)).astype(BF16)
            up_grad[cols, :] = dot_tn(rows, ups[...].reshape(total_rows, sizes.hidden)).astype(BF16)
            down_grad[:, cols] = dot_tn(
                acts[...].reshape(total_rows, sizes.hidden),
                grads[:, :, :, :, cols].reshape(total_rows, TILE),
            ).astype(BF16)

    return part


def experts_middle_kernel(
    sizes, active, own, table, gate_hbm, up_hbm, down_hbm, grads_hbm,
    out, packed_hbm, gates_hbm, ups_hbm, acts_hbm,
    gate_w, up_w, down_w, packed, grads, gates, ups, acts, load_sems, keep_sems, line, stage, *rest,
):
    buffers, gather_sems, scatter_sems = rest[:5], rest[5:10], rest[10:]
    results = buffers[0]

    @pl.when(is_section(active))
    def _():
        place = Place(sizes)
        loads = copies_of(
            ((gate_hbm, gate_w), (up_hbm, up_w), (down_hbm, down_w), (grads_hbm, grads)), load_sems
        )
        for load in loads:
            load.start()
        greet(place)
        routing = Routing(place, table)
        gather = Gather(place, routing, line, stage, packed, gather_sems)

        def compute(zz):
            @pl.when(zz == place.z)
            def _():
                for load in loads:
                    load.wait()

            rows = packed[zz].reshape(sizes.group, sizes.model)
            grad_rows = grads[zz].reshape(sizes.group, sizes.model)
            weight = routing.weights(zz)
            for f in range(sizes.hidden // TILE):
                cols = slice(f * TILE, (f + 1) * TILE)
                up = dot(rows, up_w[:, cols])
                value, slope = gelu_parts(dot(rows, gate_w[:, cols]))
                acts[zz, :, cols] = (value * up).astype(BF16)
                act_grad = dot_nt(grad_rows, down_w[cols, :]) * weight
                gates[zz, :, cols] = (act_grad * up * slope).astype(BF16)
                ups[zz, :, cols] = (act_grad * value).astype(BF16)
            store_row_grads(sizes, results, zz, gates, ups, gate_w, up_w)

        gather.run(own, compute)
        keeps = copies_of(
            ((packed, packed_hbm), (gates, gates_hbm), (ups, ups_hbm), (acts, acts_hbm)), keep_sems
        )
        for keep in keeps:
            keep.start()
        send_back(place, routing, buffers, line, out, scatter_sems, lambda j: None)
        for keep in keeps:
            keep.wait()


def experts_middle(sizes, active, normed, table, weights, grads):
    hold = Buffers(sizes)
    dma = pltpu.SemaphoreType.DMA
    return expert_call(
        functools.partial(experts_middle_kernel, sizes, active),
        2,
        (True, True, False, False, False, False),
        [
            (shape(hold.block, F32), True),
            (shape(hold.packed, BF16), False),
            (shape(hold.hidden, BF16), False),
            (shape(hold.hidden, BF16), False),
            (shape(hold.hidden, BF16), False),
        ],
        [
            pltpu.VMEM(hold.wide_weight, BF16),
            pltpu.VMEM(hold.wide_weight, BF16),
            pltpu.VMEM(hold.tall_weight, BF16),
            pltpu.VMEM(hold.packed, BF16),
            pltpu.VMEM(hold.packed, BF16),
            pltpu.VMEM(hold.hidden, BF16),
            pltpu.VMEM(hold.hidden, BF16),
            pltpu.VMEM(hold.hidden, BF16),
            dma((4,)),
            dma((4,)),
        ]
        + hold.gather
        + hold.scatter
        + hold.gather_sems
        + hold.scatter_sems,
        (normed, table, *weights, grads),
        "experts_middle",
    )


class Exchange:
    def __init__(self, sizes, partials, own, got, sums, sems):
        self.sizes, self.partials, self.own, self.got, self.sums = sizes, partials, own, got, sums
        self.own_sems, self.sent, self.come = sems
        self.axis = Axis(sizes.copies, lax.axis_index("dp"), lambda i: {"dp": i})

    def slab(self, i, y):
        at = pl.ds(pl.multiple_of(y * self.sizes.share, 128), self.sizes.share)
        return self.partials[i].at[:, at] if i == 2 else self.partials[i].at[at, :]

    def load(self, i):
        return pltpu.make_async_copy(self.slab(i, self.axis.me), self.own[i], self.own_sems.at[i])

    def sends(self):
        for i in range(3):
            for slot, peer in self.axis.peers():
                yield remote(
                    self.slab(i, peer), self.got[i].at[slot], self.sent.at[i, slot], self.come.at[i, slot],
                    self.axis.device(peer),
                )

    def keep(self, i):
        return pltpu.make_async_copy(self.own[i], self.sums[i], self.own_sems.at[i])

    def start(self):
        for i in range(3):
            self.load(i).start()
        for send in self.sends():
            send.start()

    def add(self):
        for i in range(3):
            self.load(i).wait()
            for slot, peer in self.axis.peers():
                remote(
                    self.got[i].at[slot], self.got[i].at[slot], self.sent.at[i, slot], self.come.at[i, slot],
                    self.axis.device(peer),
                ).wait_recv()
            add_rows(self.own[i], [self.got[i].at[slot] for slot, _ in self.axis.peers()], self.own[i].shape[0])
            self.keep(i).start()

    def finish(self):
        for i in range(3):
            self.keep(i).wait()
        for send in self.sends():
            send.wait_send()


def exchange_slabs(sizes):
    return [(sizes.share, sizes.hidden), (sizes.share, sizes.hidden), (sizes.hidden, sizes.share)]


def exchange_scratch(sizes):
    slabs = exchange_slabs(sizes)
    dma = pltpu.SemaphoreType.DMA
    return (
        [pltpu.VMEM(slab, BF16) for slab in slabs]
        + [pltpu.VMEM((sizes.copies - 1,) + slab, BF16) for slab in slabs]
        + [dma((3,)), dma((3, sizes.copies - 1)), dma((3, sizes.copies - 1))]
    )


def experts_after_kernel(
    sizes, active, table, down_hbm, packed_hbm, grads_hbm, gates_hbm, ups_hbm, acts_hbm,
    out, gate_sum, up_sum, down_sum,
    down_w, packed, grads, gates, ups, acts, gate_grad, up_grad, down_grad, load_sems, line, *rest,
):
    trade, buffers, scatter_sems = rest[:9], rest[9:14], rest[14:]
    results = buffers[0]

    @pl.when(is_section(active))
    def _():
        place = Place(sizes)
        loads = copies_of(
            (
                (acts_hbm, acts), (down_hbm, down_w), (packed_hbm, packed),
                (grads_hbm, grads), (gates_hbm, gates), (ups_hbm, ups),
            ),
            load_sems,
        )
        for load in loads:
            load.start()
        greet(place, [device for _, _, device in axis_peers("dp", sizes.copies)])
        routing = Routing(place, table)
        loads[0].wait()
        loads[1].wait()

        def make(zz, carry):
            weight = routing.weights(zz)
            for n in range(sizes.model // WIDE):
                cols = slice(n * WIDE, (n + 1) * WIDE)
                made = dot(acts[zz], down_w[:, cols]) * weight
                results[zz, :, :, :, cols] = made.astype(BF16).reshape(
                    sizes.width, sizes.micro, sizes.cap, WIDE
                )
            acts[zz] = (acts[zz].astype(F32) * weight).astype(BF16)
            return carry

        lax.fori_loop(0, sizes.line, make, 0)
        for load in loads[2:]:
            load.wait()
        side = weight_grads_step(sizes, packed, grads, gates, ups, acts, gate_grad, up_grad, down_grad)
        send_back(place, routing, buffers, line, out, scatter_sems, side)
        exchange = Exchange(
            sizes, (gate_grad, up_grad, down_grad), trade[:3], trade[3:6], (gate_sum, up_sum, down_sum), trade[6:]
        )
        exchange.start()
        exchange.add()
        exchange.finish()


def experts_after(sizes, active, table, down_weight, kept):
    hold = Buffers(sizes)
    return expert_call(
        functools.partial(experts_after_kernel, sizes, active),
        3,
        (True,) + (False,) * 6,
        [(shape(hold.block, F32), True)] + [(shape(slab, BF16), False) for slab in exchange_slabs(sizes)],
        [
            pltpu.VMEM(hold.tall_weight, BF16),
            pltpu.VMEM(hold.packed, BF16),
            pltpu.VMEM(hold.packed, BF16),
            pltpu.VMEM(hold.hidden, BF16),
            pltpu.VMEM(hold.hidden, BF16),
            pltpu.VMEM(hold.hidden, BF16),
            pltpu.VMEM(hold.wide_weight, BF16),
            pltpu.VMEM(hold.wide_weight, BF16),
            pltpu.VMEM(hold.tall_weight, BF16),
            pltpu.SemaphoreType.DMA((6,)),
            pltpu.VMEM(hold.lines, BF16),
        ]
        + exchange_scratch(sizes)
        + hold.scatter
        + hold.scatter_sems,
        (table, down_weight, *kept),
        "experts_after",
    )


def experts_backward_kernel(
    sizes, active, own, table, gate_hbm, up_hbm, down_hbm, packed_hbm, gates_hbm, ups_hbm,
    out, gate_grad, up_grad, down_grad,
    gate_w, up_w, down_w, packed, grads, gates, ups, acts, load_sems, line, stage, *rest,
):
    buffers, gather_sems, scatter_sems = rest[:5], rest[5:10], rest[10:]
    results = buffers[0]

    @pl.when(is_section(active))
    def _():
        place = Place(sizes)
        loads = copies_of(
            (
                (down_hbm, down_w), (gates_hbm, gates), (ups_hbm, ups),
                (gate_hbm, gate_w), (up_hbm, up_w), (packed_hbm, packed),
            ),
            load_sems,
        )
        for load in loads:
            load.start()
        greet(place)
        routing = Routing(place, table)
        gather = Gather(place, routing, line, stage, grads, gather_sems)

        def compute(zz):
            @pl.when(zz == place.z)
            def _():
                for load in loads:
                    load.wait()

            rows = grads[zz].reshape(sizes.group, sizes.model)
            weight = routing.weights(zz)
            for f in range(sizes.hidden // TILE):
                cols = slice(f * TILE, (f + 1) * TILE)
                act_grad = dot_nt(rows, down_w[cols, :]) * weight
                up = ups[zz, :, cols].astype(F32)
                value, slope = gelu_parts(gates[zz, :, cols].astype(F32))
                acts[zz, :, cols] = (value * up * weight).astype(BF16)
                gates[zz, :, cols] = (act_grad * up * slope).astype(BF16)
                ups[zz, :, cols] = (act_grad * value).astype(BF16)
            store_row_grads(sizes, results, zz, gates, ups, gate_w, up_w)

        gather.run(own, compute)
        side = weight_grads_step(sizes, packed, grads, gates, ups, acts, gate_grad, up_grad, down_grad)
        send_back(place, routing, buffers, line, out, scatter_sems, side)


def experts_backward(sizes, active, upstream, table, weights, kept):
    hold = Buffers(sizes)
    return expert_call(
        functools.partial(experts_backward_kernel, sizes, active),
        4,
        (True, True) + (False,) * 6,
        [
            (shape(hold.block, F32), True),
            (shape(hold.wide_weight, BF16), True),
            (shape(hold.wide_weight, BF16), True),
            (shape(hold.tall_weight, BF16), True),
        ],
        [
            pltpu.VMEM(hold.wide_weight, BF16),
            pltpu.VMEM(hold.wide_weight, BF16),
            pltpu.VMEM(hold.tall_weight, BF16),
            pltpu.VMEM(hold.packed, BF16),
            pltpu.VMEM(hold.packed, BF16),
            pltpu.VMEM(hold.hidden, BF16),
            pltpu.VMEM(hold.hidden, BF16),
            pltpu.VMEM(hold.hidden, BF16),
            pltpu.SemaphoreType.DMA((6,)),
        ]
        + hold.gather
        + hold.scatter
        + hold.gather_sems
        + hold.scatter_sems,
        (upstream, table, *weights, *kept),
        "experts_backward",
    )


def axis_peers(axis, count):
    me = lax.axis_index(axis)
    return [(offset, (me + offset) % count, {axis: (me + offset) % count}) for offset in range(1, count)]


def sender_of(axis, count, offset):
    return (lax.axis_index(axis) + count - offset) % count


def greet_all(devices):
    barrier = pltpu.get_barrier_semaphore()
    for device in devices:
        pl.semaphore_signal(barrier, inc=1, device_id=device, device_id_type=MESH)
    pl.semaphore_wait(barrier, len(devices))


def normalise(values, gain):
    scale = lax.rsqrt(jnp.mean(values * values, axis=-1, keepdims=True) + EPSILON)
    return values * scale * gain


def norm_backward(values, gain, grad):
    scale = lax.rsqrt(jnp.mean(values * values, axis=-1, keepdims=True) + EPSILON)
    spread = gain * grad
    inner = jnp.mean(values * spread, axis=-1, keepdims=True)
    gain_grad = jnp.sum(grad * values * scale, axis=0, keepdims=True)
    return scale * spread - values * (scale * scale * scale * inner), gain_grad


def allowed_pairs(sizes, seg_query, seg_key, m):
    offset = lax.axis_index("dp") * sizes.tokens
    shape = (sizes.tokens, sizes.seq)
    query_pos = lax.broadcasted_iota(jnp.int32, shape, 0) + offset
    key_pos = lax.broadcasted_iota(jnp.int32, shape, 1)
    return (key_pos <= query_pos) & (seg_query[m] == seg_key[m])


def stacked_heads(ref, sizes, m, g):
    rows = slice(m * sizes.tokens, (m + 1) * sizes.tokens)
    first = g * GROUPS
    return jnp.concatenate(
        [ref[rows, (first + h) * HEAD_DIM : (first + h + 1) * HEAD_DIM] for h in range(GROUPS)], axis=0
    )


def store_heads(ref, sizes, m, g, value):
    rows = slice(m * sizes.tokens, (m + 1) * sizes.tokens)
    for h in range(GROUPS):
        cols = slice((g * GROUPS + h) * HEAD_DIM, (g * GROUPS + h + 1) * HEAD_DIM)
        ref[rows, cols] = value[h * sizes.tokens : (h + 1) * sizes.tokens].astype(ref.dtype)


def softmax_parts(queries, keys, allowed, sizes):
    scores = dot_nt(queries, keys) * HEAD_DIM ** (-0.5)
    scores = scores.reshape(GROUPS, sizes.tokens, sizes.seq)
    scores = jnp.where(allowed[None], scores, MASKED).reshape(GROUPS * sizes.tokens, sizes.seq)
    powers = jnp.exp(scores - jnp.max(scores, axis=-1, keepdims=True))
    return powers, jnp.sum(powers, axis=-1, keepdims=True)


def attention_forward_kernel(
    sizes, active, x, seg_query, seg_key, attn_gain, ffn_gain, query_hbm, key_hbm, value_hbm, out_hbm,
    normed_ffn, residual, normed, queries, kv, attended,
    query_w, key_w, value_w, out_w, load_sems, kv_sent, kv_got,
):
    @pl.when(is_section(active))
    def _():
        loads = copies_of(
            ((key_hbm, key_w), (value_hbm, value_w), (query_hbm, query_w), (out_hbm, out_w)), load_sems
        )
        for load in loads:
            load.start()
        peers = axis_peers("dp", sizes.copies)
        greet_all([device for _, _, device in peers])
        normed[...] = normalise(x[...].astype(F32), attn_gain[...]).astype(BF16)
        loads[0].wait()
        loads[1].wait()
        width = KV_HEADS * HEAD_DIM
        mine = lax.axis_index("dp")
        for part, weight in enumerate((key_w, value_w)):
            made = dot(normed[...], weight[...]).astype(BF16)
            kv[:, mine, :, part * width : (part + 1) * width] = made.reshape(sizes.micro, sizes.tokens, width)
        sends = [
            remote(kv.at[:, mine], kv.at[:, mine], kv_sent.at[offset - 1], kv_got.at[offset - 1], device)
            for offset, _, device in peers
        ]
        for send in sends:
            send.start()
        loads[2].wait()
        for n in range(sizes.model // WIDE):
            cols = slice(n * WIDE, (n + 1) * WIDE)
            queries[:, cols] = dot(normed[...], query_w[:, cols]).astype(BF16)
        for offset in range(1, sizes.copies):
            theirs = sender_of("dp", sizes.copies, offset)
            block = kv.at[:, theirs]
            remote(block, block, kv_sent.at[offset - 1], kv_got.at[offset - 1], {"dp": theirs}).wait_recv()
        for m in range(sizes.micro):
            allowed = allowed_pairs(sizes, seg_query, seg_key, m)
            for g in range(KV_HEADS):
                keys = kv[m, :, :, g * HEAD_DIM : (g + 1) * HEAD_DIM].reshape(sizes.seq, HEAD_DIM)
                values = kv[m, :, :, width + g * HEAD_DIM : width + (g + 1) * HEAD_DIM]
                values = values.reshape(sizes.seq, HEAD_DIM)
                powers, sums = softmax_parts(stacked_heads(queries, sizes, m, g), keys, allowed, sizes)
                probs = (powers * (1.0 / sums)).astype(BF16)
                store_heads(attended, sizes, m, g, dot(probs, values))
        loads[3].wait()
        for n in range(sizes.model // WIDE):
            cols = slice(n * WIDE, (n + 1) * WIDE)
            residual[:, cols] = x[:, cols].astype(F32) + dot(attended[...], out_w[:, cols])
        normed_ffn[...] = normalise(residual[...], ffn_gain[...]).astype(BF16)
        for send in sends:
            send.wait_send()


def attention_forward(sizes, step, incoming, segs, gains, weights):
    rows, model = sizes.rows, sizes.model
    kv_width = KV_HEADS * HEAD_DIM
    dma = pltpu.SemaphoreType.DMA
    whole = shape((rows, model), BF16)
    kv = shape((sizes.micro, sizes.copies, sizes.tokens, 2 * kv_width), BF16)
    return pl.pallas_call(
        functools.partial(attention_forward_kernel, sizes, step),
        out_shape=[whole, shape((rows, model), F32), whole, whole, kv, whole],
        in_specs=[vmem_spec()] * 5 + [any_spec()] * 4,
        out_specs=[vmem_spec()] * 6,
        scratch_shapes=[
            pltpu.VMEM((model, model), BF16),
            pltpu.VMEM((model, kv_width), BF16),
            pltpu.VMEM((model, kv_width), BF16),
            pltpu.VMEM((model, model), BF16),
            dma((4,)),
            dma((sizes.copies - 1,)),
            dma((sizes.copies - 1,)),
        ],
        compiler_params=pltpu.CompilerParams(
            collective_id=5 + step, has_side_effects=True, vmem_limit_bytes=VMEM_BYTES
        ),
        name="attention_forward",
    )(incoming, *segs, *gains, *weights)


def attention_backward_kernel(
    sizes, active, upstream, ffn_in_grad, x, residual, queries, kv, seg_query, seg_key, attn_gain, ffn_gain,
    query_hbm, key_hbm, value_hbm, out_hbm,
    in_grad, rights, gain_grads,
    query_w, key_w, value_w, out_w, residual_grad, branch_grad, attended_grad, query_grad, kv_grad, normed_grad,
    kv_part, kv_other,
    load_sems, kv_sent, kv_got,
):
    @pl.when(is_section(active))
    def _():
        loads = [
            pltpu.make_async_copy(src, dst, load_sems.at[i])
            for i, (src, dst) in enumerate(
                ((out_hbm, out_w), (query_hbm, query_w), (key_hbm, key_w), (value_hbm, value_w))
            )
        ]
        for load in loads:
            load.start()
        peers = axis_peers("dp", sizes.copies)
        greet_all([device for _, _, device in peers])
        part, ffn_gain_grad = norm_backward(residual[...], ffn_gain[...], ffn_in_grad[...])
        total = upstream[...].astype(F32) + part
        residual_grad[...] = total
        branch_grad[...] = total.astype(BF16)
        gain_grads[...] = jnp.zeros_like(gain_grads)
        gain_grads[1:2, :] = ffn_gain_grad
        for n in range(sizes.model // WIDE):
            rights[n] = branch_grad[:, n * WIDE : (n + 1) * WIDE]
        loads[0].wait()
        for n in range(sizes.model // WIDE):
            cols = slice(n * WIDE, (n + 1) * WIDE)
            attended_grad[:, cols] = dot_nt(branch_grad[...], out_w[cols, :]).astype(BF16)
        width = KV_HEADS * HEAD_DIM
        scale = HEAD_DIM ** (-0.5)
        mine = lax.axis_index("dp")
        for m in range(sizes.micro):
            allowed = allowed_pairs(sizes, seg_query, seg_key, m)
            for g in range(KV_HEADS):
                key_cols = slice(g * HEAD_DIM, (g + 1) * HEAD_DIM)
                value_cols = slice(width + g * HEAD_DIM, width + (g + 1) * HEAD_DIM)
                keys = kv[m, :, :, key_cols].reshape(sizes.seq, HEAD_DIM)
                values = kv[m, :, :, value_cols].reshape(sizes.seq, HEAD_DIM)
                heads = stacked_heads(queries, sizes, m, g)
                grads = stacked_heads(attended_grad, sizes, m, g)
                powers, sums = softmax_parts(heads, keys, allowed, sizes)
                probs = powers * (1.0 / sums)
                probs_grad = dot_nt(grads, values)
                score_grad = probs * (probs_grad - jnp.sum(probs_grad * probs, axis=-1, keepdims=True))
                score_grad = score_grad.astype(BF16)
                value_part = dot_tn(probs.astype(BF16), grads)
                key_part = dot_tn(score_grad, heads) * scale
                store_heads(query_grad, sizes, m, g, dot(score_grad, keys) * scale)
                shape = (sizes.copies, sizes.tokens, HEAD_DIM)
                kv_part[m, :, :, key_cols] = key_part.astype(BF16).reshape(shape)
                kv_part[m, :, :, value_cols] = value_part.astype(BF16).reshape(shape)
        sends = [
            remote(kv_part.at[:, index], kv_other.at[offset - 1], kv_sent.at[offset - 1], kv_got.at[offset - 1], device)
            for offset, index, device in peers
        ]
        for send in sends:
            send.start()
        loads[1].wait()
        loads[2].wait()
        loads[3].wait()
        summed = kv_part[:, mine].astype(F32)
        for send, (offset, _, _) in zip(sends, peers):
            send.wait_recv()
            summed += kv_other[offset - 1].astype(F32)
        kv_grad[...] = summed.reshape(sizes.rows, 2 * width).astype(BF16)
        for n in range(sizes.model // WIDE):
            cols = slice(n * WIDE, (n + 1) * WIDE)
            normed_grad[:, cols] = (
                dot_nt(query_grad[...], query_w[cols, :])
                + dot_nt(kv_grad[:, :width], key_w[cols, :])
                + dot_nt(kv_grad[:, width:], value_w[cols, :])
            )
        for n in range(sizes.model // WIDE):
            rights[sizes.model // WIDE + n] = query_grad[:, n * WIDE : (n + 1) * WIDE]
        rights[2 * sizes.model // WIDE] = kv_grad[...]
        part, attn_gain_grad = norm_backward(x[...].astype(F32), attn_gain[...], normed_grad[...])
        in_grad[...] = (residual_grad[...] + part).astype(BF16)
        gain_grads[0:1, :] = attn_gain_grad
        for send in sends:
            send.wait_send()


def attention_backward(sizes, step, upstream, ffn_in_grad, x, kept, segs, gains, weights):
    rows, model = sizes.rows, sizes.model
    kv_width = KV_HEADS * HEAD_DIM
    residual, _, queries, kv, _ = kept
    dma = pltpu.SemaphoreType.DMA
    return pl.pallas_call(
        functools.partial(attention_backward_kernel, sizes, step),
        out_shape=[
            shape((rows, model), BF16),
            shape((sizes.units, rows, WIDE), BF16),
            shape((8, model), F32),
        ],
        in_specs=[vmem_spec()] * 10 + [any_spec()] * 4,
        out_specs=[vmem_spec()] * 3,
        scratch_shapes=[
            pltpu.VMEM((model, model), BF16),
            pltpu.VMEM((model, kv_width), BF16),
            pltpu.VMEM((model, kv_width), BF16),
            pltpu.VMEM((model, model), BF16),
            pltpu.VMEM((rows, model), F32),
            pltpu.VMEM((rows, model), BF16),
            pltpu.VMEM((rows, model), BF16),
            pltpu.VMEM((rows, model), BF16),
            pltpu.VMEM((rows, 2 * kv_width), BF16),
            pltpu.VMEM((rows, model), F32),
            pltpu.VMEM((sizes.micro, sizes.copies, sizes.tokens, 2 * kv_width), BF16),
            pltpu.VMEM((sizes.copies - 1, sizes.micro, sizes.tokens, 2 * kv_width), BF16),
            dma((4,)),
            dma((sizes.copies - 1,)),
            dma((sizes.copies - 1,)),
        ],
        compiler_params=pltpu.CompilerParams(
            collective_id=7 + step, has_side_effects=True, vmem_limit_bytes=VMEM_BYTES
        ),
        name="attention_backward",
    )(upstream, ffn_in_grad, x, residual, queries, kv, *segs, *gains, *weights)


class Axis:
    def __init__(self, count, me, device):
        self.count, self.me, self.device = count, me, device

    def peers(self):
        return [(offset - 1, (self.me + offset) % self.count) for offset in range(1, self.count)]

    def senders(self):
        return [(offset - 1, (self.me + self.count - offset) % self.count) for offset in range(1, self.count)]


def add_rows(dst, sources, rows):
    def step(i, carry):
        at = pl.ds(pl.multiple_of(i * 16, 16), 16)
        acc = dst[at, :].astype(F32)
        for source in sources:
            acc += source[at, :].astype(F32)
        dst[at, :] = acc.astype(BF16)
        return carry

    lax.fori_loop(0, rows // 16, step, 0)


STAGES = 5


class Reduction:
    def __init__(self, sizes, place, axes, y_first, grads, totals, crossed, lined, sems):
        self.sizes, self.place, self.grads, self.totals = sizes, place, grads, totals
        self.crossed, self.lined, self.sent, self.got = crossed, lined, sems[0], sems[1]
        along_y, along_x, along_z = axes
        self.y, self.x = along_y.me, along_x.me
        last = (along_y, along_x) if y_first else (along_x, along_y)
        self.y_first = y_first
        self.axes = (along_x, along_z, along_z) + last
        self.part = WIDE // sizes.line
        self.rows = sizes.share // sizes.width

    def piece(self, ref, z):
        return ref.at[:, pl.ds(pl.multiple_of(z * self.part, 128), self.part)]

    def gathered(self, stage, u, index):
        total = self.totals.at[u]
        if stage == 2:
            return self.piece(total.at[self.y, self.x], index)
        if stage == 3:
            return total.at[index, self.x] if self.y_first else total.at[self.y, index]
        return total.at[:, index] if self.y_first else total.at[index]

    def sends(self, stage, u):
        axis = self.axes[stage]
        for slot, peer in axis.peers():
            if stage == 0:
                source, land = self.grads.at[u, peer], self.crossed.at[u, slot]
            elif stage == 1:
                source, land = self.piece(self.grads.at[u, self.x], peer), self.lined.at[u, slot]
            else:
                source = land = self.gathered(stage, u, axis.me)
            yield remote(source, land, self.sent.at[stage, u, slot], self.got.at[stage, u, slot], axis.device(peer))

    def arrivals(self, stage, u):
        axis = self.axes[stage]
        for slot, sender in axis.senders():
            if stage == 0:
                land = self.crossed.at[u, slot]
            elif stage == 1:
                land = self.lined.at[u, slot]
            else:
                land = self.gathered(stage, u, sender)
            yield remote(land, land, self.sent.at[stage, u, slot], self.got.at[stage, u, slot], axis.device(sender))

    def start(self, stage, u):
        for copy in self.sends(stage, u):
            copy.start()

    def arrive(self, stage, u):
        for copy in self.arrivals(stage, u):
            copy.wait_recv()

    def finish(self, stage, u):
        for copy in self.sends(stage, u):
            copy.wait_send()

    def add(self, stage, u):
        if stage == 0:
            sources = [self.crossed.at[u, slot] for slot in range(self.sizes.width - 1)]
            add_rows(self.grads.at[u, self.x], sources, self.rows)
            return
        source = self.piece(self.grads.at[u, self.x], self.place.z)
        target = self.piece(self.totals.at[u, self.y, self.x], self.place.z)

        def step(i, carry):
            at = pl.ds(pl.multiple_of(i * 16, 16), 16)
            acc = source[at, :].astype(F32)
            for slot in range(self.sizes.line - 1):
                acc += self.lined[u, slot, at, :].astype(F32)
            target[at, :] = acc.astype(BF16)
            return carry

        lax.fori_loop(0, self.rows // 16, step, 0)


def reduce_kernel(sizes, active, y_first, prior, with_experts, *refs):
    refs = list(refs)
    attended, normed, rights, gains = refs[:4]
    refs = refs[4:]
    partials = []
    if with_experts:
        partials, refs = refs[:3], refs[3:]
    refs = refs[prior:]
    dense_out, gains_out, refs = refs[:3], refs[3], refs[4:]
    expert_out = []
    if with_experts:
        expert_out, refs = refs[:3], refs[3:]
    lefts_other, rights_other, grads, totals, crossed, lined, gain_sum = refs[:7]
    gain_slots, refs = refs[7:10], refs[10:]
    out_sems, gain_out_sem, left_sent, left_got, right_sent, right_got, gain_sent, gain_got, sent, got = refs[:10]
    trade = refs[10:]

    @pl.when(is_section(active))
    def _():
        place = Place(sizes)
        along_y = Axis(sizes.copies, lax.axis_index("dp"), lambda i: {"dp": i})
        along_x = Axis(sizes.width, place.x, lambda i: place.device(place.z, i))
        along_z = Axis(sizes.line, place.z, lambda i: place.device(i, place.x))
        axes = (along_y, along_x, along_z)
        greet_all([axis.device(peer) for axis in axes for _, peer in axis.peers()])
        reduction = Reduction(sizes, place, axes, y_first, grads, totals, crossed, lined, (sent, got))
        lefts = (attended, normed)
        share = sizes.share

        def left_sends(i):
            for slot, peer in along_y.peers():
                at = pl.ds(pl.multiple_of(peer * share, 128), share)
                yield remote(
                    lefts[i].at[:, at], lefts_other.at[slot, i], left_sent.at[slot, i], left_got.at[slot, i],
                    along_y.device(peer),
                )

        def right_sends(u):
            for slot, peer in along_y.peers():
                yield remote(
                    rights.at[u], rights_other.at[slot, u], right_sent.at[slot, u], right_got.at[slot, u],
                    along_y.device(peer),
                )

        def share_operands(u):
            for copy in right_sends(u):
                copy.start()

        def gain_copy(stage, slot, row, device):
            return remote(
                gain_sum.at[stage], gain_slots[stage].at[row], gain_sent.at[stage, slot], gain_got.at[stage, slot],
                device,
            )

        def gain_sends(stage):
            axis = axes[stage]
            return [gain_copy(stage, slot, axis.me, axis.device(peer)) for slot, peer in axis.peers()]

        def gain_start(stage):
            gain_slots[stage][axes[stage].me] = gain_sum[stage]
            for copy in gain_sends(stage):
                copy.start()

        def gain_end(stage):
            for slot, sender in axes[stage].senders():
                gain_copy(stage, slot, sender, axes[stage].device(sender)).wait_recv()
            acc = gain_slots[stage][0]
            for i in range(1, axes[stage].count):
                acc += gain_slots[stage][i]
            gain_sum[stage + 1] = acc

        for copy in left_sends(0):
            copy.start()
        share_operands(0)
        share_operands(1)
        for copy in left_sends(1):
            copy.start()
        gain_sum[0] = gains[...]
        gain_start(0)
        if with_experts:
            exchange = Exchange(sizes, partials, trade[:3], trade[3:6], expert_out, trade[6:])
        block = 384

        def make_from(i, u):
            @pl.when(u == i * sizes.out_units)
            def _():
                for copy in left_sends(i):
                    copy.wait_recv()

            for slot, _ in along_y.peers():
                rights_here = rights_other.at[slot, u]
                remote(
                    rights_here, rights_here, right_sent.at[slot, u], right_got.at[slot, u], along_y.device(0)
                ).wait_recv()
            for n in range(share // block):
                own = pl.ds(pl.multiple_of(along_y.me * share + n * block, 128), block)
                acc = dot_tn(lefts[i][:, own], rights[u])
                for slot, _ in along_y.peers():
                    acc += dot_tn(lefts_other[slot, i, :, n * block : (n + 1) * block], rights_other[slot, u])
                grads_rows = grads.at[u].reshape(share, WIDE)
                grads_rows[n * block : (n + 1) * block, :] = acc.astype(BF16)

        def make(u):
            @pl.when(u + 2 < sizes.units)
            def _():
                share_operands(u + 2)

            @pl.when(u < sizes.out_units)
            def _():
                make_from(0, u)

            @pl.when(u >= sizes.out_units)
            def _():
                make_from(1, u)

        rows = sizes.model

        def out_copy(u):
            source = totals.at[u].reshape(rows, WIDE)
            return source

        def each_out(u, act):
            for t, (low, high) in enumerate(((0, sizes.out_units), (sizes.out_units, sizes.units - 1))):

                @pl.when((u >= low) & (u < high))
                def _():
                    at = pl.ds(pl.multiple_of((u - low) * WIDE, WIDE), WIDE)
                    act(pltpu.make_async_copy(out_copy(u), dense_out[t].at[:, at], out_sems.at[u]))

            @pl.when(u == sizes.units - 1)
            def _():
                act(pltpu.make_async_copy(out_copy(u), dense_out[2], out_sems.at[u]))

        def tick_body(tick, carry):
            for stage in range(STAGES, -1, -1):
                u = tick - stage

                @pl.when((u >= 0) & (u < sizes.units))
                def _():
                    if stage == 0:
                        make(u)
                    else:
                        reduction.arrive(stage - 1, u)
                        if stage <= 2:
                            reduction.add(stage - 1, u)
                    if stage < STAGES:
                        reduction.start(stage, u)
                    else:
                        each_out(u, lambda copy: copy.start())

            for stage in range(3):

                @pl.when(tick == stage)
                def _():
                    gain_end(stage)
                    if stage < 2:
                        gain_start(stage + 1)

            if with_experts:

                @pl.when(tick == sizes.units - 1)
                def _():
                    exchange.start()

            return carry

        lax.fori_loop(0, sizes.units + STAGES, tick_body, 0)
        gains_copy = pltpu.make_async_copy(gain_sum.at[3], gains_out, gain_out_sem)
        gains_copy.start()
        if with_experts:
            exchange.add()

        def finish(u, carry):
            for stage in range(STAGES):
                reduction.finish(stage, u)
            for copy in right_sends(u):
                copy.wait_send()
            each_out(u, lambda copy: copy.wait())
            return carry

        lax.fori_loop(0, sizes.units, finish, 0)
        for i in range(2):
            for copy in left_sends(i):
                copy.wait_send()
        for stage in range(3):
            for copy in gain_sends(stage):
                copy.wait_send()
        gains_copy.wait()
        if with_experts:
            exchange.finish()


def reduce_grads(sizes, active, y_first, operands, experts, prior):
    model, copies, width, line = sizes.model, sizes.copies, sizes.width, sizes.line
    units, rows, share = sizes.units, sizes.rows, sizes.share
    with_experts = len(experts) > 0
    dma = pltpu.SemaphoreType.DMA
    outs = [shape((model, model), BF16), shape((model, model), BF16), shape((model, WIDE), BF16)]
    outs.append(shape((8, model), F32))
    if with_experts:
        outs += [shape(slab, BF16) for slab in exchange_slabs(sizes)]
    most = max(copies, width, line) - 1
    scratch = [
        pltpu.VMEM((copies - 1, 2, rows, share), BF16),
        pltpu.VMEM((copies - 1, units, rows, WIDE), BF16),
        pltpu.VMEM((units, width, share // width, WIDE), BF16),
        pltpu.VMEM((units, copies, width, share // width, WIDE), BF16),
        pltpu.VMEM((units, width - 1, share // width, WIDE), BF16),
        pltpu.VMEM((units, line - 1, share // width, WIDE // line), BF16),
        pltpu.VMEM((4, 8, model), F32),
    ]
    scratch += [pltpu.VMEM((count, 8, model), F32) for count in (copies, width, line)]
    scratch += [dma((units,)), dma, dma((copies - 1, 2)), dma((copies - 1, 2))]
    scratch += [dma((copies - 1, units)), dma((copies - 1, units)), dma((3, most)), dma((3, most))]
    scratch += [dma((STAGES, units, most)), dma((STAGES, units, most))]
    if with_experts:
        scratch += exchange_scratch(sizes)
    return pl.pallas_call(
        functools.partial(reduce_kernel, sizes, active, y_first, len(prior), with_experts),
        out_shape=outs,
        in_specs=[vmem_spec()] * 4 + [any_spec()] * (len(experts) + len(prior)),
        out_specs=[any_spec()] * len(outs),
        scratch_shapes=scratch,
        input_output_aliases={4 + len(experts) + i: i for i in range(len(prior))},
        compiler_params=pltpu.CompilerParams(
            collective_id=9 + active, has_side_effects=True, vmem_limit_bytes=VMEM_BYTES
        ),
        name="reduce_grads",
    )(*operands, *experts, *prior)


def routing_table(sizes, expert_ids, route_weights):
    named = expert_ids[None] == jnp.arange(sizes.experts, dtype=jnp.int32)[:, None, None, None]
    used = jnp.any(named, axis=-1)
    weight = jnp.sum(jnp.where(named, route_weights[None], 0.0), axis=-1)
    before = jnp.triu(jnp.ones((sizes.tokens, sizes.tokens), BF16), 1)
    rank = jnp.where(used, dot(used.astype(BF16), before), -1.0)
    return jnp.stack([rank, weight], axis=2)


def per_device(
    boundary, w_query, w_key, w_value, w_out, norm_attn, norm_ffn, w_gate, w_up, w_down,
    expert_ids, route_weights, segments,
):
    micro, tokens, model = boundary.shape[1:]
    sizes = Sizes(lax.axis_size("expert"), lax.axis_size("dp"), micro, tokens, model, w_gate.shape[-1])
    first = lax.axis_index("section") == 0
    weights = (w_query[0], w_key[0], w_value[0], w_out[0])
    gains = (norm_attn, norm_ffn)
    expert_params = (w_gate[0, 0], w_up[0, 0], w_down[0, 0])
    own_table = routing_table(sizes, expert_ids[0], route_weights[0])
    offset = lax.axis_index("dp") * tokens
    query_seg = lax.dynamic_slice_in_dim(segments, offset, tokens, axis=1)
    segs = (query_seg[:, :, None], segments[:, None, :])
    own_rows = boundary[0].reshape(sizes.rows, model)

    def blocks(rows):
        return rows.reshape(micro, tokens, model)

    def flat(value):
        return value.reshape(sizes.rows, model)

    def attention_grads(step, upstream, ffn_in_grad, incoming, stored):
        residual, normed, queries, kv, attended = stored
        in_grad, rights, gain_grads = attention_backward(
            sizes, step, upstream, flat(ffn_in_grad), incoming, stored, segs, gains, weights
        )
        return in_grad, (attended, normed, rights, gain_grads)

    table, grad_rows = begin(sizes, 1, blocks(own_rows), own_table)
    normed_ffn, *stored_0 = attention_forward(sizes, 0, own_rows, segs, gains, weights)
    mixed, *kept_0 = experts_forward(sizes, 0, blocks(normed_ffn), table, expert_params)
    out_0 = (stored_0[0] + flat(mixed)).astype(BF16)
    received = lax.ppermute(out_0, "section", [(0, 1)])
    normed_ffn, *stored_1 = attention_forward(sizes, 1, received, segs, gains, weights)
    ffn_in_grad, packed_rows, *kept_1 = experts_middle(
        sizes, 1, blocks(normed_ffn), table, expert_params, grad_rows
    )
    in_grad_1, dense_1 = attention_grads(1, own_rows, ffn_in_grad, received, stored_1)
    upstream_0 = lax.ppermute(in_grad_1, "section", [(1, 0)])
    dense_sums = reduce_grads(sizes, 1, False, dense_1, (), ())
    packed_rows, dense_sums = lax.optimization_barrier((packed_rows, tuple(dense_sums)))
    mixed, *expert_sums = experts_after(sizes, 1, table, expert_params[2], (packed_rows, grad_rows, *kept_1))
    out_1 = (stored_1[0] + flat(mixed)).astype(BF16)
    ffn_in_grad, *expert_0 = experts_backward(sizes, 0, blocks(upstream_0), table, expert_params, kept_0)
    in_grad_0, dense_0 = attention_grads(0, upstream_0, ffn_in_grad, own_rows, stored_0)
    sums = reduce_grads(sizes, 0, True, dense_0, expert_0, (*dense_sums, *expert_sums))

    def choose(a, b):
        return jnp.where(first, a, b).reshape(1, micro, tokens, model)

    kv_width = KV_HEADS * HEAD_DIM
    out_sum, query_sum, kv_sum, gain_sum, gate_sum, up_sum, down_sum = sums
    return (
        choose(out_0, out_1),
        choose(in_grad_0, in_grad_1),
        query_sum.astype(F32)[None],
        kv_sum[:, :kv_width].astype(F32)[None],
        kv_sum[:, kv_width:].astype(F32)[None],
        out_sum.astype(F32)[None],
        gain_sum[0][None],
        gain_sum[1][None],
        gate_sum.astype(F32)[None, None],
        up_sum.astype(F32)[None, None],
        down_sum.astype(F32)[None, None],
    )


def solution(mesh):
    in_specs = (
        P("section", None, ("expert", "dp"), None),
        P("section", None, None),
        P("section", None, None),
        P("section", None, None),
        P("section", None, None),
        P("section", None),
        P("section", None),
        P("section", "expert", None, None),
        P("section", "expert", None, None),
        P("section", "expert", None, None),
        P("section", None, ("expert", "dp"), None),
        P("section", None, ("expert", "dp"), None),
        P(None, "expert"),
    )
    out_specs = (
        P("section", None, ("expert", "dp"), None),
        P("section", None, ("expert", "dp"), None),
        P("section", None, None),
        P("section", None, None),
        P("section", None, None),
        P("section", None, None),
        P("section", None),
        P("section", None),
        P("section", "expert", "dp", None),
        P("section", "expert", "dp", None),
        P("section", "expert", None, "dp"),
    )
    return jax.shard_map(
        per_device, mesh=mesh, in_specs=in_specs, out_specs=out_specs, check_vma=False
    )
```
